128 devices in a mesh: row: 32 (over y, z, x_hi), col: 4 (over x_lo, core).
Axes of the slice: x: 4 (x_hi: 2, x_lo: 2; x = x_hi * 2 + x_lo), y: 4, z: 4, core: 2. Of those that a mesh axis runs over, the one named last changes fastest.
Arguments:
- hidden_in: bfloat16 [16384, 1024], P('row', 'col'), may hold values from -6 to 6
- segment_ids: int32 [16384], P('row'), may hold values from 0 to 3, as said below
- cotangent: bfloat16 [16384, 1024], P('row', 'col'), may hold values from -6 to 6
- w_in: bfloat16 [1, 1024, 4120], P(None, 'row', 'col'), may hold values from -0.1875 to 0.1875
- w_out: bfloat16 [1, 2048, 1024], P(None, 'col', 'row'), may hold values from -0.1875 to 0.1875
- w_gate_up: bfloat16 [1, 1024, 4096], P(None, 'row', 'col'), may hold values from -0.1875 to 0.1875
- w_down: bfloat16 [1, 2048, 1024], P(None, 'col', 'row'), may hold values from -0.125 to 0.125
- norm_gains: float32 [1, 2, 1024], P(None, None, 'col'), may hold values from 0.5 to 1.5
- ssm_gain: float32 [1, 1536], P(None, 'col'), may hold values from 0.5 to 1.5
- head_params: float32 [1, 3, 24], P(None, None, 'col'), may hold values from -7 to 3
- conv_weight: float32 [1, 4, 1792], P(None, None, 'col'), may hold values from -3 to 3
- conv_bias: float32 [1, 1792], P(None, 'col'), may hold values from -3 to 3
Outputs:
- hidden_out: bfloat16 [16384, 1024], P('row', 'col')
- grad_hidden: float32 [16384, 1024], P('row', 'col')
- grad_w_in: float32 [1, 1024, 4120], P(None, 'row', 'col')
- grad_w_out: float32 [1, 2048, 1024], P(None, 'col', 'row')
- grad_w_gate_up: float32 [1, 1024, 4096], P(None, 'row', 'col')
- grad_w_down: float32 [1, 2048, 1024], P(None, 'col', 'row')
- grad_norm_gains: float32 [1, 2, 1024], P(None, None, 'col')
- grad_ssm_gain: float32 [1, 1536], P(None, 'col')
- grad_head_params: float32 [1, 3, 24], P(None, None, 'col')
- grad_conv_weight: float32 [1, 4, 1792], P(None, None, 'col')
- grad_conv_bias: float32 [1, 1792], P(None, 'col')
The draws below stay inside these ranges and needn't reach their ends.
Inputs may be any that keep to these rules, and one draw needn't show every extreme that they name: `segment_ids`: within each sequence of 512 tokens the ids start at 0, never fall, rise by one at each step up, and end at 3.
All inputs are finite; a program needn't handle non-finite values.
Results may differ from the reference program's by a relative error of at most 0.024.
Values may be sent and summed in bfloat16 or wider, within the bound.
No kernel may reach another device: no remote copies, remote signals or barrier semaphores. Data moves between devices by JAX's collectives and lax.ppermute only.
A program may use at most 128 MiB of HBM per device.

```python
import jax
import jax.numpy as jnp
from jax import lax

D = 1024
Q_HEADS = 8
KV_HEADS = 2
HEAD = 64
SSM_HEADS = 24
SSM_HEAD = 64
STATE = 128
CONV = 4
FF = 2048
LAYERS = 1
SEQ = 512
TOKENS = 16384
IN = 4120
MIX = 2048
CONVCH = 1792
N_ROW = 32
N_COL = 4


def cuts_of_one(key):
    order = jax.random.permutation(key, SEQ - 1)[:3] + 1
    index = jnp.arange(SEQ, dtype=jnp.int32)
    marks = jnp.any(index[:, None] == order[None, :].astype(jnp.int32), axis=1)
    return jnp.cumsum(marks.astype(jnp.int32)).astype(jnp.int32)


def draw_segment_ids(key, part):
    key = jax.random.fold_in(key, 11)
    keys = jax.random.split(key, TOKENS // SEQ)
    return jax.vmap(cuts_of_one)(keys).reshape(TOKENS).astype(jnp.int32)


def draw_head_params(key, part):
    key = jax.random.fold_in(key, 23)
    first, second, third = jax.random.split(key, 3)
    shape = (LAYERS, SSM_HEADS)
    rate_log = jnp.log(jax.random.uniform(first, shape, jnp.float32, 1.0, 16.0))
    skip = jax.random.uniform(second, shape, jnp.float32, 0.5, 1.5)
    step_size = jnp.exp(jax.random.uniform(third, shape, jnp.float32, jnp.log(0.001), jnp.log(0.1)))
    step_bias = jnp.log(jnp.expm1(step_size))
    return jnp.stack([rate_log, skip, step_bias], axis=1)


def levels(own_key, shape, pieces, low, high):
    factor_of = 1.0
    for dim, blocks in pieces:
        steps = jax.random.uniform(jax.random.fold_in(jax.random.fold_in(own_key, 6), dim), (blocks,), jnp.float32, low / len(pieces), high / len(pieces))
        factor_of = factor_of * jnp.repeat(jnp.exp(steps), shape[dim] // blocks).reshape((-1,) + (1,) * (len(shape) - 1 - dim))
    return factor_of


def gaussian(rng, dims, spread, bound, pieces=(), held_as=jnp.bfloat16):
    array = spread * jax.random.normal(rng, dims, jnp.float32)
    if pieces:
        array = array * levels(rng, dims, pieces, -0.22, 0.18)
    return jnp.clip(array, -bound, bound).astype(held_as)


def setup_inputs(seed: int = 0) -> dict:
    streams_of = jax.random.split(jax.random.key(seed), 13)
    return {
        "hidden_in": gaussian(streams_of[0], (TOKENS, D), 1.0, 6.0, ((0, 32), (1, 4))),
        "segment_ids": draw_segment_ids(jax.random.fold_in(streams_of[12], 71), 0),
        "cotangent": gaussian(streams_of[2], (TOKENS, D), 1.0, 6.0, ((0, 32), (1, 4))),
        "w_in": gaussian(streams_of[3], (LAYERS, D, IN), D ** -0.5, 0.1875, ((1, 32), (2, 4))),
        "w_out": gaussian(streams_of[4], (LAYERS, MIX, D), (MIX // 2) ** -0.5, 0.1875, ((1, 4), (2, 32))),
        "w_gate_up": gaussian(streams_of[5], (LAYERS, D, 2 * FF), D ** -0.5, 0.1875, ((1, 32), (2, 4))),
        "w_down": gaussian(streams_of[6], (LAYERS, FF, D), FF ** -0.5, 0.125, ((1, 4), (2, 32))),
        "norm_gains": jnp.clip(1.0 + 0.1 * jax.random.normal(streams_of[7], (LAYERS, 2, D), jnp.float32), 0.5, 1.5),
        "ssm_gain": jnp.clip(1.0 + 0.1 * jax.random.normal(streams_of[8], (LAYERS, SSM_HEADS * SSM_HEAD), jnp.float32), 0.5, 1.5),
        "head_params": draw_head_params(jax.random.fold_in(streams_of[12], 71), 0),
        "conv_weight": gaussian(streams_of[10], (LAYERS, CONV, CONVCH), 0.5, 3.0, ((2, 4),), jnp.float32),
        "conv_bias": gaussian(streams_of[11], (LAYERS, CONVCH), 0.5, 3.0, ((1, 4),), jnp.float32),
    }


epsilon = 1e-05
rope_base = 10000.0
highest = lax.Precision.HIGHEST

@jax.custom_vjp
def low(v):
    return lax.optimization_barrier(v.astype(jnp.bfloat16)).astype(jnp.float32)

@jax.custom_vjp
def low_back(v):
    return v

def low_keep(v):
    return (low(v), None)

def low_pass(kept, grad):
    return (grad,)

def back_keep(v):
    return (v, None)

def back_low(kept, grad):
    return (low(grad),)
low.defvjp(low_keep, low_pass)
low_back.defvjp(back_keep, back_low)

def matmul(left, right):
    return jnp.dot(left, right, precision=highest)

def rms_scale(values):
    return lax.rsqrt(lax.optimization_barrier(jnp.mean(values * values, axis=-1, keepdims=True)) + epsilon)

def sequence_masks(segments):
    length = segments.shape[0]
    index = jnp.arange(length, dtype=jnp.int32)
    previous = jnp.concatenate([segments[:1], segments[:-1]])
    starts = jnp.where(segments != previous, index, 0)
    positions = (index - lax.cummax(starts, axis=0)).astype(jnp.float32)
    allowed = (segments[:, None] == segments[None, :]) & (index[:, None] >= index[None, :])
    shifted = []
    for shift in range(CONV):
        earlier = jnp.concatenate([jnp.full((shift,), -1, jnp.int32), segments[:length - shift]])
        shifted.append((earlier == segments).astype(jnp.float32))
    return (positions, allowed, jnp.stack(shifted))

def rotate(values, positions):
    middle = values.shape[-1] // 2
    frequency = rope_base ** (-2.0 * jnp.arange(middle, dtype=jnp.float32) / values.shape[-1])
    angle = positions[:, None] * frequency[None, :]
    cosine = jnp.cos(angle)[:, None, :]
    sine = jnp.sin(angle)[:, None, :]
    first = values[..., :middle]
    second = values[..., middle:]
    return jnp.concatenate([first * cosine - second * sine, second * cosine + first * sine], -1)

def causal_conv(inner, weight, bias, valid):
    length = inner.shape[0]
    running = jnp.broadcast_to(bias[None, :], inner.shape)
    for shift in range(CONV):
        earlier = jnp.concatenate([jnp.zeros((shift, inner.shape[1]), inner.dtype), inner[:length - shift]])
        running = running + weight[shift][None, :] * earlier * valid[shift][:, None]
    return running

def layer_forward(resid, positions, allowed, valid, w_in, w_out, w_gate_up, w_down, gains, ssm_gain, heads, conv_weight, conv_bias):
    query_cols = Q_HEADS * HEAD // N_COL
    ssm_cols = SSM_HEADS * SSM_HEAD // N_COL
    state_cols = 2 * STATE // N_COL
    block_cols = query_cols + 2 * ssm_cols + HEAD + state_cols + SSM_HEADS // N_COL
    start_kv = query_cols + 2 * ssm_cols
    length = resid.shape[0]
    normed = low(resid * rms_scale(resid) * gains[0])
    proj = low_back(matmul(normed, w_in)).reshape(length, N_COL, block_cols)
    query = proj[:, :, :query_cols].reshape(length, Q_HEADS, HEAD)
    gate_z = proj[:, :, query_cols:query_cols + ssm_cols].reshape(length, N_COL * ssm_cols)
    inner = jnp.concatenate([proj[:, :, query_cols + ssm_cols:start_kv], proj[:, :, start_kv + HEAD:start_kv + HEAD + state_cols]], 2)
    inner = inner.reshape(length, N_COL * (ssm_cols + state_cols))
    convolved = jax.nn.silu(causal_conv(inner, conv_weight, conv_bias, valid)).reshape(length, N_COL, ssm_cols + state_cols)
    xin = convolved[:, :, :ssm_cols].reshape(length, SSM_HEADS, SSM_HEAD)
    states = low(convolved[:, :, ssm_cols:].reshape(length, 2 * STATE))
    state_b = states[:, :STATE]
    state_c = states[:, STATE:]
    keyval = low(proj[:, :, start_kv:start_kv + HEAD])
    keys = keyval[:, :KV_HEADS]
    values = keyval[:, KV_HEADS:]
    step_raw = proj[:, :, start_kv + HEAD + state_cols:].reshape(length, SSM_HEADS)
    group = Q_HEADS // KV_HEADS
    qrot = low(rotate(query, positions))
    krot = jnp.repeat(low(rotate(keys, positions)), group, axis=1)
    vrep = jnp.repeat(values, group, axis=1)
    scores = jnp.einsum('shd,thd->hst', qrot, krot, precision=highest) * HEAD ** (-0.5)
    scores = jnp.where(allowed[None], scores, -1e+30)
    top = lax.optimization_barrier(jnp.max(scores, axis=-1, keepdims=True))
    weights = jnp.exp(scores - top)
    probs = low(weights / lax.optimization_barrier(jnp.sum(weights, axis=-1, keepdims=True)))
    attn = low(jnp.einsum('hst,thd->shd', probs, vrep, precision=highest)).reshape(length, N_COL, query_cols)
    step_size = jax.nn.softplus(step_raw + heads[2][None, :])
    logdecay = jnp.cumsum(step_size * (-jnp.exp(heads[0]))[None, :], axis=0).T
    gram = matmul(state_c, state_b.T)
    diff = logdecay[:, :, None] - logdecay[:, None, :]
    mixing = low(jnp.where(allowed[None], jnp.exp(jnp.where(allowed[None], diff, 0.0)), 0.0) * gram[None])
    inputs = low(step_size[:, :, None] * xin)
    ssm = jnp.einsum('hts,shp->thp', mixing, inputs, precision=highest) + heads[1][None, :, None] * xin
    gated = ssm.reshape(length, SSM_HEADS * SSM_HEAD) * jax.nn.silu(gate_z)
    sout = low(gated * rms_scale(gated) * ssm_gain).reshape(length, N_COL, ssm_cols)
    mixed = jnp.concatenate([attn, sout], 2).reshape(length, MIX)
    resid = resid + low_back(matmul(mixed, w_out))
    normed_two = low(resid * rms_scale(resid) * gains[1])
    gate_up = low_back(matmul(normed_two, w_gate_up)).reshape(length, N_COL, 2, FF // N_COL)
    hidden = low(jax.nn.silu(gate_up[:, :, 0]) * gate_up[:, :, 1]).reshape(length, FF)
    return resid + low_back(matmul(hidden, w_down))

def reference(hidden_in, segment_ids, cotangent, w_in, w_out, w_gate_up, w_down, norm_gains, ssm_gain, head_params, conv_weight, conv_bias):
    params = (w_in.astype(jnp.float32), w_out.astype(jnp.float32), w_gate_up.astype(jnp.float32), w_down.astype(jnp.float32), norm_gains, ssm_gain, head_params, conv_weight, conv_bias)

    def forward(resid, segments, weights):
        positions, allowed, valid = sequence_masks(segments)
        for layer_index in range(LAYERS):
            resid = layer_forward(resid, positions, allowed, valid, *(item[layer_index] for item in weights))
        return resid
    inputs = hidden_in.astype(jnp.float32).reshape(N_ROW, SEQ, D)
    segments_all = segment_ids.reshape(N_ROW, SEQ)
    grads_in = cotangent.astype(jnp.float32).reshape(N_ROW, SEQ, D)

    def step(totals, item):
        start_x, segments, upstream = item
        result, pull = jax.vjp(lambda value, weights: forward(value, segments, weights), start_x, params)
        grad_x, grad_params = pull(upstream)
        return (jax.tree.map(jnp.add, totals, grad_params), (result, grad_x))
    zeros = jax.tree.map(jnp.zeros_like, params)
    totals, (results, grad_x) = lax.scan(step, zeros, (inputs, segments_all, grads_in))
    return (results.reshape(TOKENS, D).astype(jnp.bfloat16), grad_x.reshape(TOKENS, D), totals[0], totals[1], totals[2], totals[3], totals[4], totals[5], totals[6], totals[7], totals[8])
```

```python
import jax
import jax.numpy as jnp
from jax import lax
from jax.sharding import PartitionSpec as P

D = 1024
Q_HEADS = 8
KV_HEADS = 2
HEAD = 64
SSM_HEADS = 24
SSM_HEAD = 64
STATE = 128
CONV = 4
FF = 2048
LAYERS = 1


epsilon = 1e-05
rope_base = 10000.0
contract_last = (((1,), (1,)), ((), ()))
contract_first = (((0,), (0,)), ((), ()))


def lowered(value):
    rounded = lax.optimization_barrier(value.astype(jnp.bfloat16)).astype(jnp.float32)
    return value + lax.stop_gradient(rounded - value)


def sequence_masks(segments):
    length = segments.shape[0]
    index = jnp.arange(length, dtype=jnp.int32)
    previous = jnp.concatenate([segments[:1], segments[:-1]])
    starts = jnp.where(segments != previous, index, 0)
    positions = (index - lax.cummax(starts, axis=0)).astype(jnp.float32)
    allowed = (segments[:, None] == segments[None, :]) & (index[:, None] >= index[None, :])
    shifted = []
    for shift in range(CONV):
        earlier = jnp.concatenate([jnp.full((shift,), -1, jnp.int32), segments[: length - shift]])
        shifted.append((earlier == segments).astype(jnp.float32))
    return (positions, allowed, jnp.stack(shifted))


def rotate(values, positions):
    middle = values.shape[-1] // 2
    frequency = rope_base ** (-2.0 * jnp.arange(middle, dtype=jnp.float32) / values.shape[-1])
    angle = positions[:, None] * frequency[None, :]
    cosine = jnp.cos(angle)[:, None, :]
    sine = jnp.sin(angle)[:, None, :]
    first = values[..., :middle]
    second = values[..., middle:]
    return jnp.concatenate([first * cosine - second * sine, second * cosine + first * sine], -1)


def causal_conv(inner, weight, bias, valid):
    length = inner.shape[0]
    running = jnp.broadcast_to(bias[None, :], inner.shape)
    for shift in range(CONV):
        earlier = jnp.concatenate(
            [jnp.zeros((shift, inner.shape[1]), inner.dtype), inner[: length - shift]]
        )
        running = running + weight[shift][None, :] * earlier * valid[shift][:, None]
    return running


def conv_section(block, weight, bias, valid, widths):
    query_cols, ssm_cols, state_cols, head_cols = widths
    start_kv = query_cols + 2 * ssm_cols
    inner = jnp.concatenate(
        [
            block[:, query_cols + ssm_cols : start_kv],
            block[:, start_kv + HEAD : start_kv + HEAD + state_cols],
        ],
        1,
    )
    active = jax.nn.silu(causal_conv(inner, weight, bias, valid))
    sent = jnp.concatenate(
        [lowered(block[:, start_kv : start_kv + HEAD]), lowered(active[:, ssm_cols:])], 1
    )
    return (active[:, :ssm_cols], sent)


def split_shared(shared, column, widths):
    query_cols, ssm_cols, state_cols, head_cols = widths
    length = shared.shape[0]
    col_count = shared.shape[1] // (HEAD + state_cols)
    pieces = shared.reshape(length, col_count, HEAD + state_cols)
    key_index = column * KV_HEADS // col_count
    keys = lax.dynamic_index_in_dim(pieces[:, :KV_HEADS, :HEAD], key_index, 1, keepdims=False)
    values = lax.dynamic_index_in_dim(pieces[:, KV_HEADS:, :HEAD], key_index, 1, keepdims=False)
    states = pieces[:, :, HEAD:].reshape(length, col_count * state_cols)
    return (keys, values, states)


def attention_core(block, shared, positions, allowed, column, widths):
    query_cols, ssm_cols, state_cols, head_cols = widths
    length = block.shape[0]
    keys, values, states = split_shared(shared, column, widths)
    query = block[:, :query_cols].reshape(length, query_cols // HEAD, HEAD)
    qrot = lowered(rotate(query, positions))
    krot = lowered(rotate(keys[:, None, :], positions))[:, 0]
    scores = jnp.einsum("shd,td->hst", qrot, krot) * HEAD ** (-0.5)
    scores = jnp.where(allowed[None], scores, -1e30)
    top = jnp.max(scores, axis=-1, keepdims=True)
    weights = jnp.exp(scores - top)
    probs = lowered(weights / jnp.sum(weights, axis=-1, keepdims=True))
    return lowered(jnp.einsum("hst,td->shd", probs, values)).reshape(length, query_cols)


def ssm_core(block, convolved, shared, params, allowed, column, widths):
    query_cols, ssm_cols, state_cols, head_cols = widths
    length = block.shape[0]
    keys, values, states = split_shared(shared, column, widths)
    state_b = states[:, :STATE]
    state_c = states[:, STATE:]
    gate_z = block[:, query_cols : query_cols + ssm_cols]
    step_size = jax.nn.softplus(block[:, block.shape[1] - head_cols :] + params[2][None, :])
    logdecay = jnp.cumsum(step_size * (-jnp.exp(params[0]))[None, :], axis=0).T
    gram = jnp.dot(state_c, state_b.T)
    diff = logdecay[:, :, None] - logdecay[:, None, :]
    mixing = lowered(
        jnp.where(allowed[None], jnp.exp(jnp.where(allowed[None], diff, 0.0)), 0.0) * gram[None]
    )
    xin = convolved.reshape(length, head_cols, SSM_HEAD)
    inputs = lowered(step_size[:, :, None] * xin)
    ssm = jnp.einsum("hts,shp->thp", mixing, inputs) + params[1][None, :, None] * xin
    return ssm.reshape(length, ssm_cols) * jax.nn.silu(gate_z)


def swap_core(values):
    return lax.ppermute(values, "col", [(0, 1), (1, 0), (2, 3), (3, 2)])


def swap_chip(values):
    return lax.ppermute(values, "col", [(0, 2), (2, 0), (1, 3), (3, 1)])


def sum_col(values):
    values = values + swap_core(values)
    return values + swap_chip(values)


def gather_features(block, chip, core):
    other = swap_chip(block)
    pair = jnp.stack([jnp.where(chip == 0, block, other), jnp.where(chip == 0, other, block)])
    opair = swap_core(pair)
    even = jnp.where(core == 0, pair, opair)
    odd = jnp.where(core == 0, opair, pair)
    return jnp.concatenate([even[0], odd[0], even[1], odd[1]], 1)


def feature_sum(partial, chip, core):
    width = partial.shape[1] // 4
    blocks = [partial[:, i * width : (i + 1) * width] for i in range(4)]
    even = jnp.stack([blocks[0], blocks[2]])
    odd = jnp.stack([blocks[1], blocks[3]])
    sent = jnp.where(core == 0, odd, even).astype(jnp.bfloat16)
    pair = jnp.where(core == 0, even, odd) + swap_core(sent).astype(jnp.float32)
    sent = jnp.where(chip == 0, pair[1], pair[0]).astype(jnp.bfloat16)
    return jnp.where(chip == 0, pair[0], pair[1]) + swap_chip(sent).astype(jnp.float32)


def token_half(values, core):
    half = values.shape[0] // 2
    return jnp.where(core == 0, values[:half], values[half:])


def token_sum(partial, core):
    sent = token_half(partial, 1 - core).astype(jnp.bfloat16)
    pair = token_half(partial, core) + swap_core(sent).astype(jnp.float32)
    return pair + swap_chip(pair.astype(jnp.bfloat16)).astype(jnp.float32)


def token_spread(half, core):
    other = swap_core(half)
    return jnp.concatenate([jnp.where(core == 0, half, other), jnp.where(core == 0, other, half)], 0)


def per_device(
    hidden_in,
    segment_ids,
    cotangent,
    w_in,
    w_out,
    w_gate_up,
    w_down,
    norm_gains,
    ssm_gain,
    head_params,
    conv_weight,
    conv_bias,
):
    rows = lax.axis_size("row")
    col_count = lax.axis_size("col")
    column = lax.axis_index("col")
    chip = column // 2
    core = column % 2
    widths = (
        Q_HEADS * HEAD // col_count,
        SSM_HEADS * SSM_HEAD // col_count,
        2 * STATE // col_count,
        SSM_HEADS // col_count,
    )
    query_cols, ssm_cols, state_cols, head_cols = widths
    ffn_cols = FF // col_count
    ssm_width = SSM_HEADS * SSM_HEAD
    shard = w_in.shape[1]
    in_cols = w_in.shape[2]
    mix_cols = w_out.shape[1]
    bf16 = jnp.bfloat16
    f32 = jnp.float32

    def mm(left, right, dims):
        return lax.dot_general(left, right, dims, preferred_element_type=f32)

    plain = (((1,), (0,)), ((), ()))

    spread = jnp.broadcast_to(w_in[0][None], (rows, shard, in_cols))
    w_in_full = lax.all_to_all(spread, "row", 0, 0, tiled=True).reshape(rows * shard, in_cols)
    rest = jnp.concatenate([w_out[0].T, w_gate_up[0], w_down[0].T], 1)
    rest = lax.all_gather(rest, "row", axis=0, tiled=True)
    w_out_t = rest[:, :mix_cols]
    w_gu = rest[:, mix_cols : mix_cols + 2 * ffn_cols]
    w_down_t = rest[:, mix_cols + 2 * ffn_cols :]

    positions, allowed, valid = sequence_masks(segment_ids)
    gains = gather_features(norm_gains[0], chip, core)
    source = gather_features(hidden_in, chip, core).astype(f32)
    scale_one = lax.rsqrt(jnp.mean(source * source, axis=1, keepdims=True) + epsilon)
    normed = (source * scale_one * gains[0][None, :]).astype(bf16)
    upstream = gather_features(cotangent, chip, core)

    block = mm(normed, w_in_full, plain)

    def section(block_in, weight_in, bias_in):
        return conv_section(block_in, weight_in, bias_in, valid, widths)

    (convolved, sent), pull_section = jax.vjp(section, block, conv_weight[0], conv_bias[0])
    shared = gather_features(sent.astype(bf16), chip, core).astype(f32)

    def ssm(block_in, conv_in, shared_in, params_in):
        return ssm_core(block_in, conv_in, shared_in, params_in, allowed, column, widths)

    gated, pull_ssm = jax.vjp(ssm, block, convolved, shared, head_params[0])
    ssq = sum_col(jnp.sum(gated * gated, axis=1))

    def attention(block_in, shared_in):
        return attention_core(block_in, shared_in, positions, allowed, column, widths)

    attn, pull_attn = jax.vjp(attention, block, shared)
    scale_ssm = lax.rsqrt(ssq / ssm_width + epsilon)
    sout = gated * scale_ssm[:, None] * ssm_gain[0][None, :]
    mixed = jnp.concatenate([attn, sout], 1).astype(bf16)

    after_mix = token_half(source, core) + token_sum(mm(mixed, w_out_t, contract_last), core)
    scale_two = lax.rsqrt(jnp.mean(after_mix * after_mix, axis=1, keepdims=True) + epsilon)
    normed_two = token_spread((after_mix * scale_two * gains[1][None, :]).astype(bf16), core)
    gate_up = mm(normed_two, w_gu, plain)
    gate = gate_up[:, :ffn_cols]
    upper = gate_up[:, ffn_cols:]
    sigmoid = jax.nn.sigmoid(gate)
    activated = (gate * sigmoid * upper).astype(bf16)

    half_features = jnp.arange(D) // (D // 2) == chip
    kept = jnp.where(half_features[None, :], after_mix, 0.0)
    none = jnp.zeros_like(kept)
    placed = jnp.concatenate([jnp.where(core == 0, kept, none), jnp.where(core == 0, none, kept)], 0)
    hidden_out = feature_sum(mm(activated, w_down_t, contract_last) + placed, chip, core)

    grad_act = mm(upstream, w_down_t, plain)
    grad_down_t = mm(upstream, activated, contract_first)
    grad_gate = grad_act * upper * sigmoid * (1.0 + gate * (1.0 - sigmoid))
    grad_up = grad_act * gate * sigmoid
    grad_gu = jnp.concatenate([grad_gate, grad_up], 1).astype(bf16)
    partial_two = token_sum(mm(grad_gu, w_gu, contract_last), core)
    grad_w_gu = mm(normed_two, grad_gu, contract_first)
    scaled = partial_two * gains[1][None, :]
    inner = jnp.sum(scaled * after_mix, axis=1, keepdims=True)
    grad_mid = (
        token_half(upstream, core).astype(f32)
        + scale_two * scaled
        - after_mix * (scale_two**3 * inner / D)
    )
    gain_two = jnp.sum(partial_two * after_mix * scale_two, axis=0)
    gain_two = gain_two + swap_core(gain_two)
    upstream_two = token_spread(grad_mid.astype(bf16), core)

    grad_mixed = mm(upstream_two, w_out_t, plain)
    grad_out_t = mm(upstream_two, mixed, contract_first)
    grad_attn = grad_mixed[:, :query_cols]
    grad_sout = grad_mixed[:, query_cols:]
    scaled = grad_sout * ssm_gain[0][None, :]
    inner = sum_col(jnp.sum(scaled * gated, axis=1))
    grad_block_attn, grad_shared_attn = pull_attn(grad_attn)
    grad_gated = scale_ssm[:, None] * scaled - gated * (scale_ssm**3 * inner / ssm_width)[:, None]
    grad_ssm_gain = jnp.sum(grad_sout * gated * scale_ssm[:, None], axis=0)
    grad_block_ssm, grad_conv, grad_shared_ssm, grad_heads = pull_ssm(grad_gated)
    grad_sent = feature_sum(grad_shared_attn + grad_shared_ssm, chip, core)
    grad_block_conv, grad_cweight, grad_cbias = pull_section((grad_conv, grad_sent))
    grad_block = (grad_block_attn + grad_block_ssm + grad_block_conv).astype(bf16)

    partial_one = mm(grad_block, w_in_full, contract_last)
    scaled = partial_one * gains[0][None, :]
    inner = jnp.sum(scaled * source, axis=1, keepdims=True)
    kept = jnp.where(half_features[None, :], grad_mid, 0.0)
    placed = jnp.concatenate([jnp.where(core == 0, kept, none), jnp.where(core == 0, none, kept)], 0)
    grad_hidden = feature_sum(
        scale_one * scaled - source * (scale_one**3 * inner / D) + placed, chip, core
    )
    gain_one = jnp.sum(partial_one * source * scale_one, axis=0)
    gain_one = sum_col(gain_one)
    grad_w_in = mm(normed, grad_block, contract_first)

    own = lax.dynamic_slice_in_dim(jnp.stack([gain_one, gain_two]), column * (D // 4), D // 4, 1)
    pieces = (own, grad_ssm_gain, grad_heads, grad_cweight, grad_cbias)
    flat = jnp.concatenate([piece.reshape(-1) for piece in pieces])
    pad_cols = -in_cols % 128
    flat = jnp.pad(flat, (0, shard * pad_cols - flat.shape[0])).astype(bf16).reshape(shard, pad_cols)
    small = jnp.broadcast_to(flat[None], (rows, shard, pad_cols)).reshape(rows * shard, pad_cols)
    packed = jnp.concatenate(
        [
            grad_out_t.astype(bf16),
            grad_w_gu.astype(bf16),
            grad_down_t.astype(bf16),
            grad_w_in.astype(bf16),
            small,
        ],
        1,
    ).reshape(rows, shard, -1)
    packed = lax.all_to_all(packed, "row", 0, 0, tiled=True)
    total = jnp.sum(packed.astype(f32), axis=0)
    gu_end = mix_cols + 2 * ffn_cols
    down_end = gu_end + ffn_cols
    flat = total[:, down_end + in_cols :].reshape(-1)
    out_small = []
    start = 0
    for piece in pieces:
        out_small.append(flat[start : start + piece.size].reshape((1,) + piece.shape))
        start += piece.size
    return (
        hidden_out.astype(bf16),
        grad_hidden,
        total[None, :, down_end : down_end + in_cols],
        total[:, :mix_cols].T[None],
        total[None, :, mix_cols:gu_end],
        total[:, gu_end:down_end].T[None],
        *out_small,
    )


def solution(mesh):
    in_specs = (
        P("row", "col"),
        P("row"),
        P("row", "col"),
        P(None, "row", "col"),
        P(None, "col", "row"),
        P(None, "row", "col"),
        P(None, "col", "row"),
        P(None, None, "col"),
        P(None, "col"),
        P(None, None, "col"),
        P(None, None, "col"),
        P(None, "col"),
    )
    out_specs = (
        P("row", "col"),
        P("row", "col"),
        P(None, "row", "col"),
        P(None, "col", "row"),
        P(None, "row", "col"),
        P(None, "col", "row"),
        P(None, None, "col"),
        P(None, "col"),
        P(None, None, "col"),
        P(None, None, "col"),
        P(None, "col"),
    )
    return jax.shard_map(
        per_device, mesh=mesh, in_specs=in_specs, out_specs=out_specs, check_vma=False
    )
```

```python
import math

import jax
import jax.numpy as jnp
from jax import lax
from jax.experimental import pallas as pl
from jax.experimental.pallas import tpu as pltpu
from jax.sharding import PartitionSpec as P

D = 1024
Q_HEADS = 8
KV_HEADS = 2
HEAD = 64
SSM_HEADS = 24
SSM_HEAD = 64
STATE = 128
CONV = 4
FF = 2048
LAYERS = 1
CHUNK = 256
VMEM_BYTES = 60 * 1024 * 1024


epsilon = 1e-05
rope_base = 10000.0
contract_last = (((1,), (1,)), ((), ()))
contract_first = (((0,), (0,)), ((), ()))


def sequence_masks(segments):
    length = segments.shape[0]
    index = jnp.arange(length, dtype=jnp.int32)
    previous = jnp.concatenate([segments[:1], segments[:-1]])
    starts = jnp.where(segments != previous, index, 0)
    positions = (index - lax.cummax(starts, axis=0)).astype(jnp.float32)
    allowed = (segments[:, None] == segments[None, :]) & (index[:, None] >= index[None, :])
    shifted = []
    for shift in range(CONV):
        earlier = jnp.concatenate([jnp.full((shift,), -1, jnp.int32), segments[: length - shift]])
        shifted.append((earlier == segments).astype(jnp.float32))
    return (positions, allowed, jnp.stack(shifted))


def where_lane(shape, limit):
    return lax.broadcasted_iota(jnp.int32, shape, 1) < limit


def sigmoid(values):
    return 1.0 / (1.0 + jnp.exp(-values))


def softplus(values):
    return jnp.maximum(values, 0.0) + jnp.log1p(jnp.exp(-jnp.abs(values)))


def four_blocks(idx, own, by_chip, by_core, by_both):
    chip0 = idx[0] == 0
    core0 = idx[1] == 0
    first = jnp.where(chip0, own, by_chip)
    second = jnp.where(chip0, by_core, by_both)
    third = jnp.where(chip0, by_chip, own)
    fourth = jnp.where(chip0, by_both, by_core)
    return (
        jnp.where(core0, first, second),
        jnp.where(core0, second, first),
        jnp.where(core0, third, fourth),
        jnp.where(core0, fourth, third),
    )


def rotated(values, cosine, sine):
    lane = lax.broadcasted_iota(jnp.int32, values.shape, 1)
    other = jnp.where(lane % HEAD < HEAD // 2, pltpu.roll(values, 96, 1), pltpu.roll(values, 32, 1))
    return values * cosine + other * sine


def conv_pre(inner, weight, bias, valid):
    running = bias + weight[0:1] * inner * valid[:, 0:1]
    for shift in range(1, CONV):
        running = running + weight[shift : shift + 1] * pltpu.roll(inner, shift, 0) * valid[
            :, shift : shift + 1
        ]
    return running


def conv_back(grad, inner, weight, valid):
    length = inner.shape[0]
    total = weight[0:1] * (grad * valid[:, 0:1])
    taps = [jnp.sum(grad * valid[:, 0:1] * inner, axis=0, keepdims=True)]
    for shift in range(1, CONV):
        seen = grad * valid[:, shift : shift + 1]
        total = total + weight[shift : shift + 1] * pltpu.roll(seen, length - shift, 0)
        taps.append(jnp.sum(seen * pltpu.roll(inner, shift, 0), axis=0, keepdims=True))
    return (total, taps, jnp.sum(grad, axis=0, keepdims=True))


def silu_slope(values, sig):
    return sig * (1.0 + values * (1.0 - sig))


def dot32(left, right, dims=(((1,), (0,)), ((), ()))):
    return lax.dot_general(left, right, dims, preferred_element_type=jnp.float32)


def exact(left, right):
    return lax.dot_general(
        left,
        right,
        (((1,), (0,)), ((), ())),
        precision=lax.Precision.HIGHEST,
        preferred_element_type=jnp.float32,
    )


def triangle(length, reverse=False):
    first = lax.broadcasted_iota(jnp.int32, (length, length), 0)
    second = lax.broadcasted_iota(jnp.int32, (length, length), 1)
    return jnp.where(second >= first if reverse else first >= second, 1.0, 0.0)


def head_sums(width):
    lane = lax.broadcasted_iota(jnp.int32, (width, 128), 0) // SSM_HEAD
    head = lax.broadcasted_iota(jnp.int32, (width, 128), 1)
    return jnp.where(lane == head, 1.0, 0.0)


def per_head(columns, tile, shape):
    return jnp.where(
        where_lane(shape, SSM_HEAD),
        jnp.broadcast_to(columns[:, 2 * tile : 2 * tile + 1], shape),
        jnp.broadcast_to(columns[:, 2 * tile + 1 : 2 * tile + 2], shape),
    )


def chunk_allowed(tok, seg, start, count):
    rows = tok.shape[0]
    time = lax.broadcasted_iota(jnp.int32, (rows, count), 0) + start
    source = lax.broadcasted_iota(jnp.int32, (rows, count), 1)
    return (tok[:, 4:5] == seg[0:1, :count]) & (time >= source)


def table_kernel(seg, params, tok_out, cosine_out, sine_out, heads_out, skip_out):
    length = seg.shape[1]
    shape = (length, 128)
    column = row_to_column(seg[...])
    time = lax.broadcasted_iota(jnp.int32, (length, 1), 0)
    allowed = chunk_allowed(jnp.broadcast_to(column, (length, 8)), seg[...], 0, length)
    positions = jnp.sum(jnp.where(allowed, 1.0, 0.0), axis=1, keepdims=True) - 1.0
    lane = lax.broadcasted_iota(jnp.int32, shape, 1)
    wide = jnp.broadcast_to(column, shape)
    tok = jnp.where(lane == 4, wide, 0.0)
    for shift in range(CONV):
        same = wide == (pltpu.roll(wide, shift, 0) if shift else wide)
        tok = jnp.where((lane == shift) & same & (time >= shift), 1.0, tok)
    tok_out[...] = tok
    slot = (lane % (HEAD // 2)).astype(jnp.float32)
    angle = positions * jnp.exp(slot * (-2.0 * math.log(rope_base) / HEAD))
    cosine_out[...] = jnp.cos(angle)
    sine = jnp.sin(angle)
    sine_out[...] = jnp.where(lane % HEAD < HEAD // 2, -sine, sine)
    heads_out[...] = jnp.zeros(heads_out.shape, jnp.float32)
    heads_out[0:3, 0:6] = params[...]
    lane = lax.broadcasted_iota(jnp.int32, skip_out.shape, 1) // SSM_HEAD
    skip = jnp.zeros(skip_out.shape, jnp.float32)
    for head in range(params.shape[1]):
        skip = jnp.where(lane == head, params[1:2, head : head + 1], skip)
    skip_out[...] = skip


def in_kernel(
    idx, own, by_chip, by_core, by_both, gain, weight, cweight, cbias, tok,
    normed_out, scale_out, proj_out, xin_out, sent_out,
):
    source = jnp.concatenate(
        four_blocks(idx, own[...], by_chip[...], by_core[...], by_both[...]), 1
    ).astype(jnp.float32)
    scale = lax.rsqrt(jnp.sum(source * source, axis=1, keepdims=True) / D + epsilon)
    normed = (source * scale * gain[0:1]).astype(jnp.bfloat16)
    normed_out[...] = normed
    scale_out[...] = scale
    proj = dot32(normed, weight[...])
    proj_out[...] = proj
    inner = proj[:, 512:1024]
    pre = conv_pre(inner, cweight[...], cbias[0:1], tok[...])
    active = pre * sigmoid(pre)
    xin_out[...] = active[:, :384]
    tile = inner[:, 384:]
    sent_out[...] = jnp.where(where_lane(tile.shape, HEAD), tile, active[:, 384:]).astype(
        jnp.bfloat16
    )


def mixer_kernel(
    idx, proj, xin, own, by_chip, by_core, by_both, tok, seg, cosine, sine, heads, skip,
    attn_out, gated_out, ssm_out, ssq_out, probs_out, qrot_out, krot_out, value_out,
    state_b_out, state_c_out, step_out, cumc_out, cumr_out,
):
    f32 = jnp.float32
    bf16 = jnp.bfloat16
    length = proj.shape[0]
    blocks = four_blocks(
        idx, own[...].astype(f32), by_chip[...].astype(f32), by_core[...].astype(f32),
        by_both[...].astype(f32),
    )
    chip0 = idx[0] == 0
    shape = (length, 128)
    left = where_lane(shape, HEAD)
    keys = jnp.where(chip0, blocks[0], blocks[1])
    values = jnp.where(chip0, blocks[2], blocks[3])
    keys = jnp.where(left, keys, pltpu.roll(keys, 64, 1))
    values = jnp.where(left, values, pltpu.roll(values, 64, 1)).astype(bf16)
    state_b = jnp.where(left, pltpu.roll(blocks[0], 64, 1), blocks[1]).astype(bf16)
    state_c = jnp.where(left, pltpu.roll(blocks[2], 64, 1), blocks[3]).astype(bf16)
    krot = rotated(keys, cosine[...], sine[...]).astype(bf16)
    qrot = rotated(proj[:, :128], cosine[...], sine[...]).astype(bf16)
    value_out[...] = values
    state_b_out[...] = state_b
    state_c_out[...] = state_c
    krot_out[...] = krot
    qrot_out[...] = qrot
    step = softplus(proj[:, 1024:1152] + heads[2:3])
    step_out[...] = step
    cum = exact(triangle(length), step * -jnp.exp(heads[0:1]))
    cumc_out[...] = cum
    cumr = cum.T[:8]
    cumr_out[...] = cumr
    xin_all = xin[...]
    tiles = xin_all.shape[1] // 128
    inputs = [
        (per_head(step, tile, shape) * xin_all[:, 128 * tile : 128 * tile + 128]).astype(bf16)
        for tile in range(tiles)
    ]
    half = min(CHUNK, length)
    for start in range(0, length, half):
        count = start + half
        rows = slice(start, count)
        allowed = chunk_allowed(tok[rows, :], seg[...], start, count)
        first = where_lane((half, 128), HEAD)
        outs = []
        for head in range(2):
            query = jnp.where(first == (head == 0), qrot[rows].astype(f32), 0.0).astype(bf16)
            scores = dot32(query, krot[:count], contract_last) * HEAD ** (-0.5)
            scores = jnp.where(allowed, scores, -1e30)
            weights = jnp.exp(scores - jnp.max(scores, axis=1, keepdims=True))
            probs = (weights / jnp.sum(weights, axis=1, keepdims=True)).astype(bf16)
            probs_out[head, rows, :count] = probs
            outs.append(dot32(probs, values[:count]))
        attn_out[rows, :] = jnp.where(first, outs[0], outs[1]).astype(bf16)
        gram = dot32(state_c[rows], state_b[:count], contract_last)
        total = jnp.zeros((half, 128), f32)
        for tile in range(tiles):
            lanes = slice(128 * tile, 128 * tile + 128)
            outs = []
            for head in (2 * tile, 2 * tile + 1):
                diff = cum[rows, head : head + 1] - cumr[head : head + 1, :count]
                mixing = jnp.exp(jnp.where(allowed, diff, -1e30)) * gram
                outs.append(dot32(mixing.astype(bf16), inputs[tile][:count]))
            ssm = jnp.where(first, outs[0], outs[1]) + skip[0:1, lanes] * xin_all[rows, lanes]
            ssm_out[rows, lanes] = ssm
            gate = proj[rows, 128 + 128 * tile : 256 + 128 * tile]
            gated = ssm * (gate * sigmoid(gate))
            gated_out[rows, lanes] = gated
            total = total + gated * gated
        ssq_out[:, rows] = lax.dot_general(
            jnp.ones((8, 128), f32),
            total,
            contract_last,
            precision=lax.Precision.HIGHEST,
            preferred_element_type=f32,
        )


def attention_back_kernel(
    grad, attn, probs, qrot, krot, value, cosine, sine, tok,
    dquery_out, dkey_out, dvalue_out,
):
    f32 = jnp.float32
    bf16 = jnp.bfloat16
    length = grad.shape[0]
    shape = (length, 128)
    lane0 = where_lane(shape, HEAD)
    dkey = [jnp.zeros(shape, f32), jnp.zeros(shape, f32)]
    dvalue = jnp.zeros(shape, f32)
    half = min(CHUNK, length)
    dquery = []
    keyparts = []
    valueparts = []
    for start in range(0, length, half):
        count = start + half
        rows = slice(start, count)
        first = where_lane((half, 128), HEAD)
        dout = grad[rows, :]
        product = dout * attn[rows, :].astype(f32)
        outs = []
        dk = []
        dv = []
        for head in range(2):
            mine = first == (head == 0)
            dhead = jnp.where(mine, dout, 0.0).astype(bf16)
            query = jnp.where(mine, qrot[rows, :].astype(f32), 0.0).astype(bf16)
            part = probs[head, rows, :count]
            dprob = dot32(dhead, value[:count, :], contract_last)
            inner = jnp.sum(jnp.where(mine, product, 0.0), axis=1, keepdims=True)
            dscore = (part.astype(f32) * (dprob - inner) * HEAD ** (-0.5)).astype(bf16)
            outs.append(dot32(dscore, krot[:count, :]))
            dk.append(dot32(dscore, query, contract_first))
            dv.append(dot32(part, dhead, contract_first))
        dquery.append(jnp.where(first, outs[0], outs[1]))
        keyparts.append(dk[0] + dk[1])
        valueparts.append(dv[0] + dv[1])

    def gathered(parts):
        total = parts[-1]
        for part in parts[:-1]:
            pad = jnp.zeros((length - part.shape[0], 128), f32)
            total = total + jnp.concatenate([part, pad], 0)
        return total + pltpu.roll(total, 64, 1)

    back = -sine[...]
    dquery_out[...] = rotated(jnp.concatenate(dquery, 0), cosine[...], back).astype(bf16)
    dkey_out[...] = rotated(gathered(keyparts), cosine[...], back)
    dvalue_out[...] = gathered(valueparts)


def ssm_back_kernel(
    idx, scaled, gated, ssm, scale_ssm, inner, dquery, proj, xin, step, cumc, cumr, state_b, state_c,
    tok, seg, heads, skip, cweight, cbias, dkey, dvalue,
    dproj_out, keep_out, send_out, small_out, conv_out,
):
    f32 = jnp.float32
    bf16 = jnp.bfloat16
    length = proj.shape[0]
    shape = (length, 128)
    tiles = xin.shape[1] // 128
    scale = scale_ssm[...]
    shrink = scale * scale * scale * row_to_column(inner[...]) / (SSM_HEADS * SSM_HEAD)
    dproj_out[:, :128] = dquery[...]
    dproj_out[:, 896:1024] = jnp.zeros((length, 128), bf16)
    step_all = step[...]
    left = where_lane(shape, HEAD)
    grads = []
    grads_low = []
    inputs = []
    for tile in range(tiles):
        lanes = slice(128 * tile, 128 * tile + 128)
        gate = proj[:, 128 + 128 * tile : 256 + 128 * tile]
        sig = sigmoid(gate)
        grad_gated = scale * scaled[:, lanes] - gated[:, lanes] * shrink
        dproj_out[:, 128 + 128 * tile : 256 + 128 * tile] = (grad_gated * ssm[:, lanes] * silu_slope(gate, sig)).astype(bf16)
        grad = grad_gated * gate * sig
        grads.append(grad)
        grads_low.append(grad.astype(bf16))
        inputs.append((per_head(step_all, tile, shape) * xin[:, lanes]).astype(bf16))
    half = min(CHUNK, length)
    dinputs = [[] for _ in range(tiles)]
    dstate_b = []
    dstate_c = []
    for start in range(0, length, half):
        count = start + half
        rows = slice(start, count)
        allowed = chunk_allowed(tok[rows, :], seg[...], start, count)
        first = where_lane((half, 128), HEAD)
        gram = dot32(state_c[rows, :], state_b[:count, :], contract_last)
        dgram = jnp.zeros((half, count), f32)
        for tile in range(tiles):
            pair = []
            low = grads_low[tile][rows]
            for head in (2 * tile, 2 * tile + 1):
                diff = cumc[rows, head : head + 1] - cumr[head : head + 1, :count]
                decay = jnp.exp(jnp.where(allowed, diff, -1e30))
                mixing = (decay * gram).astype(bf16)
                mine = jnp.where(first == (head % 2 == 0), low.astype(f32), 0.0).astype(bf16)
                dgram = dgram + decay * dot32(mine, inputs[tile][:count], contract_last)
                pair.append(dot32(mixing, low, contract_first))
            dinputs[tile].append(jnp.where(where_lane((count, 128), HEAD), pair[0], pair[1]))
        dgram = dgram.astype(bf16)
        dstate_c.append(dot32(dgram, state_b[:count, :]))
        dstate_b.append(dot32(dgram, state_c[rows, :], contract_first))

    def gathered(parts):
        total = parts[-1]
        for part in parts[:-1]:
            pad = jnp.zeros((length - part.shape[0], 128), f32)
            total = total + jnp.concatenate([part, pad], 0)
        return total

    valid = tok[...]
    balance = jnp.zeros(shape, f32)
    dstep = jnp.zeros(shape, f32)
    dskip = jnp.zeros((1, 128), f32)
    sums = head_sums(128 * tiles)
    for tile in range(tiles):
        lanes = slice(128 * tile, 128 * tile + 128)
        dinput = gathered(dinputs[tile])
        own = xin[:, lanes]
        plain = ssm[:, lanes] - skip[0:1, lanes] * own
        select = sums[128 * tile : 128 * tile + 128]
        balance = balance + exact(
            grads_low[tile].astype(f32) * plain - inputs[tile].astype(f32) * dinput, select
        )
        dstep = dstep + exact(dinput * own, select)
        dskip = dskip + exact(
            jnp.broadcast_to(jnp.sum(grads[tile] * own, axis=0, keepdims=True), (8, 128)), select
        )[0:1]
        dxin = skip[0:1, lanes] * grads[tile] + per_head(step_all, tile, shape) * dinput
        source = proj[:, 512 + 128 * tile : 640 + 128 * tile]
        weight = cweight[:, lanes]
        pre = conv_pre(source, weight, cbias[0:1, lanes], valid)
        dpre = dxin * silu_slope(pre, sigmoid(pre))
        dsource, taps, dbias = conv_back(dpre, source, weight, valid)
        dproj_out[:, 512 + 128 * tile : 640 + 128 * tile] = dsource.astype(bf16)
        for shift in range(CONV):
            conv_out[shift : shift + 1, lanes] = taps[shift]
        conv_out[CONV : CONV + 1, lanes] = dbias
    rate = -jnp.exp(heads[0:1])
    dlog = exact(triangle(length, True), balance)
    dstep = (dstep + dlog * rate) * sigmoid(proj[:, 1024:1152] + heads[2:3])
    dstep = jnp.where(where_lane(shape, SSM_HEADS // 4), dstep, 0.0)
    dproj_out[:, 1024:] = dstep.astype(bf16)
    small_out[0:1, :] = jnp.sum(dlog * step_all, axis=0, keepdims=True) * rate
    small_out[1:2, :] = dskip
    small_out[2:3, :] = jnp.sum(dstep, axis=0, keepdims=True)
    small_out[3:8, :] = jnp.zeros((5, 128), f32)
    dstate_b = gathered(dstate_b)
    dstate_c = jnp.concatenate(dstate_c, 0)
    chip0 = idx[0] == 0
    core0 = idx[1] == 0
    none = jnp.zeros(shape, f32)
    dkey0 = jnp.where(chip0, dkey[...], none)
    dkey1 = jnp.where(chip0, none, dkey[...])
    dvalue0 = jnp.where(chip0, dvalue[...], none)
    dvalue1 = jnp.where(chip0, none, dvalue[...])
    pieces = (
        jnp.where(left, dkey0, pltpu.roll(dstate_b, 64, 1)),
        jnp.where(left, dkey1, dstate_b),
        jnp.where(left, dvalue0, pltpu.roll(dstate_c, 64, 1)),
        jnp.where(left, dvalue1, dstate_c),
    )
    near = (jnp.where(core0, pieces[0], pieces[1]), jnp.where(core0, pieces[2], pieces[3]))
    away = (jnp.where(core0, pieces[1], pieces[0]), jnp.where(core0, pieces[3], pieces[2]))
    keep_out[0, :, :] = jnp.where(chip0, near[0], near[1])
    keep_out[1, :, :] = jnp.where(chip0, near[1], near[0])
    send_out[0, :, :] = jnp.where(chip0, away[0], away[1]).astype(bf16)
    send_out[1, :, :] = jnp.where(chip0, away[1], away[0]).astype(bf16)


def row_to_column(row):
    return jnp.broadcast_to(row[0:1], (128, row.shape[1])).T[:, 0:1]


def half_rows(core, length):
    return pl.ds(pl.multiple_of(core * (length // 2), length // 2), length // 2)


def mix_kernel(idx, attn, gated, total, gain, weight, mixed_out, scale_out, keep_out, send_out):
    length = attn.shape[0]
    scale = lax.rsqrt(row_to_column(total[...]) / (SSM_HEADS * SSM_HEAD) + epsilon)
    scale_out[...] = scale
    mixed_out[:, :128] = attn[...]
    mixed_out[:, 128:] = (gated[...] * scale * gain[0:1]).astype(jnp.bfloat16)
    core = idx[1]
    near = mixed_out[half_rows(core, length), :]
    away = mixed_out[half_rows(1 - core, length), :]
    send_out[...] = dot32(away, weight[...], contract_last).astype(jnp.bfloat16)
    keep_out[...] = dot32(near, weight[...], contract_last)


def block_halves(idx, blocks):
    rows = half_rows(idx[1], blocks[0].shape[0])
    return jnp.concatenate(four_blocks(idx, *(block[rows, :] for block in blocks)), 1).astype(
        jnp.float32
    )


def norm_kernel(idx, own, by_chip, by_core, by_both, pair, got, gain, after_out, scale_out, low_out):
    after = (
        block_halves(idx, (own, by_chip, by_core, by_both))
        + pair[...]
        + got[...].astype(jnp.float32)
    )
    scale = lax.rsqrt(jnp.sum(after * after, axis=1, keepdims=True) / D + epsilon)
    after_out[...] = after
    scale_out[...] = scale
    low_out[...] = (after * scale * gain[0:1]).astype(jnp.bfloat16)


def joined(idx, near, away):
    core0 = idx[1] == 0
    near, away = near[...], away[...]
    return jnp.concatenate([jnp.where(core0, near, away), jnp.where(core0, away, near)], 0)


def mlp_kernel(
    idx, near, away, own, by_chip, by_core, by_both, weights,
    normed_out, up_out, act_out, grad_out, keep_out, send_out,
):
    length = own.shape[0]
    cols = weights.shape[1] // 3
    w_gu = weights.at[:, : 2 * cols]
    w_down = weights.at[:, 2 * cols :]
    normed = joined(idx, near, away)
    normed_out[...] = normed
    upstream = jnp.concatenate(
        four_blocks(idx, own[...], by_chip[...], by_core[...], by_both[...]), 1
    )
    up_out[...] = upstream
    both = dot32(normed, w_gu[...])
    gate = both[:, :cols]
    upper = both[:, cols:]
    sig = sigmoid(gate)
    act_out[...] = (gate * sig * upper).astype(jnp.bfloat16)
    grad = dot32(upstream, w_down[...])
    grad_out[:, :cols] = (grad * upper * silu_slope(gate, sig)).astype(jnp.bfloat16)
    grad_out[:, cols:] = (grad * gate * sig).astype(jnp.bfloat16)
    core = idx[1]
    away = grad_out[half_rows(1 - core, length), :]
    send_out[...] = dot32(away, w_gu[...], contract_last).astype(jnp.bfloat16)
    keep_out[...] = dot32(grad_out[half_rows(core, length), :], w_gu[...], contract_last)


def norm_back_kernel(
    idx, own, by_chip, by_core, by_both, pair, got, after, scale, gain, grad_out, low_out, gain_out
):
    partial = pair[...] + got[...].astype(jnp.float32)
    source = after[...]
    r = scale[...]
    scaled = partial * gain[0:1]
    inner = jnp.sum(scaled * source, axis=1, keepdims=True)
    grad = (
        block_halves(idx, (own, by_chip, by_core, by_both))
        + r * scaled
        - source * (r * r * r * inner / D)
    )
    grad_out[...] = grad
    low_out[...] = grad.astype(jnp.bfloat16)
    gain_out[...] = jnp.sum(partial * source * r, axis=0, keepdims=True)


def mix_back_kernel(
    idx, near, away, weight, gated, scale, gain, up_out, attn_out, scaled_out, inner_out, gain_out
):
    upstream = joined(idx, near, away)
    up_out[...] = upstream
    grad = dot32(upstream, weight[...])
    attn_out[...] = grad[:, :128]
    grad = grad[:, 128:]
    scaled = grad * gain[0:1]
    scaled_out[...] = scaled
    source = gated[...]
    product = scaled * source
    inner_out[...] = lax.dot_general(
        jnp.ones((8, product.shape[1]), jnp.float32),
        product,
        contract_last,
        precision=lax.Precision.HIGHEST,
        preferred_element_type=jnp.float32,
    )
    gain_out[...] = jnp.sum(grad * source * scale[...], axis=0, keepdims=True)


def feature_blocks(idx, total, keep_out, send_out):
    chip, core = idx[0], idx[1]
    for place, way in ((0, chip), (1, 1 - chip)):
        near = pl.multiple_of((2 * way + core) * 256, 256)
        away = pl.multiple_of((2 * way + 1 - core) * 256, 256)
        keep_out[place, :, :] = total[:, pl.ds(near, 256)]
        send_out[place, :, :] = total[:, pl.ds(away, 256)].astype(jnp.bfloat16)


def add_residual(idx, total, resid):
    rows = half_rows(idx[1], total.shape[0])
    lanes = pl.ds(pl.multiple_of(idx[0] * (D // 2), D // 2), D // 2)
    total[rows, lanes] = total[rows, lanes] + resid[:, lanes]


def down_kernel(idx, act, weight, resid, keep_out, send_out, total):
    total[...] = dot32(act[...], weight[:, 1024:], contract_last)
    add_residual(idx, total, resid)
    feature_blocks(idx, total, keep_out, send_out)


def in_back_kernel(
    idx, dproj, dsent, proj, tok, cweight, cbias, weight, own, by_chip, by_core, by_both,
    scale, gain, grad_mid, late_out, conv_out, gain_out, keep_out, send_out, total,
):
    inner = proj[:, 896:1024]
    taps_in = cweight[:, 384:]
    valid = tok[...]
    pre = conv_pre(inner, taps_in, cbias[0:1, 384:], valid)
    grad = dsent[...]
    dpre = grad * silu_slope(pre, sigmoid(pre))
    dinner, taps, dbias = conv_back(dpre, inner, taps_in, valid)
    for shift in range(CONV):
        conv_out[shift : shift + 1, :] = taps[shift]
    conv_out[CONV : CONV + 1, :] = dbias
    tile = jnp.where(where_lane(grad.shape, HEAD), grad, dinner).astype(jnp.bfloat16)
    late_out[...] = dproj[...]
    late_out[:, 896:1024] = tile
    partial = dot32(late_out[...], weight[...], contract_last)
    source = jnp.concatenate(
        four_blocks(idx, own[...], by_chip[...], by_core[...], by_both[...]), 1
    ).astype(jnp.float32)
    r = scale[...]
    scaled = partial * gain[0:1]
    dots = jnp.sum(scaled * source, axis=1, keepdims=True)
    total[...] = r * scaled - source * (r * r * r * dots / D)
    gain_out[...] = jnp.sum(partial * source * r, axis=0, keepdims=True)
    add_residual(idx, total, grad_mid)
    feature_blocks(idx, total, keep_out, send_out)


def grads_kernel(first, second, third, fourth, out):
    cols = second.shape[1]
    more = out.shape[1] - cols
    out[:, :cols] = dot32(first[...], second[...], contract_first).astype(jnp.bfloat16)
    out[:, cols:] = dot32(third[...], fourth[:, :more], contract_first).astype(jnp.bfloat16)


def last_grads_kernel(up, mixed, normed, dproj, small, out):
    cols = mixed.shape[1]
    out[:, :cols] = dot32(up[...], mixed[...], contract_first).astype(jnp.bfloat16)
    out[:, cols:] = dot32(normed[...], dproj[...], contract_first).astype(jnp.bfloat16)
    shard = small.shape[0]
    first = where_lane((shard, 128), 6)
    for start in range(0, out.shape[0], shard):
        rows = slice(start, start + shard)
        out[rows, cols + 1024 :] = jnp.where(
            first, out[rows, cols + 1024 :].astype(jnp.float32), small[...].astype(jnp.float32)
        ).astype(jnp.bfloat16)


def call(body, outs, *args, scratch=(), flops=0, exps=0):
    moved = sum(a.size * a.dtype.itemsize for a in args)
    moved += sum(math.prod(s) * jnp.dtype(t).itemsize for s, t in outs)
    scalars = sum(a.dtype == jnp.int32 for a in args)
    arrays = args[scalars:]
    n_in, n_out = len(arrays), len(outs)

    def kernel(*refs):
        first = refs[:scalars]
        refs = refs[scalars:]
        far_in, far_out = refs[:n_in], refs[n_in : n_in + n_out]
        refs = refs[n_in + n_out :]
        near_in, near_out = refs[:n_in], refs[n_in : n_in + n_out]
        *rest, sems = refs[n_in + n_out :]
        fetches = [
            pltpu.make_async_copy(far, near, sems.at[i])
            for i, (far, near) in enumerate(zip(far_in, near_in))
        ]
        for copy in fetches:
            copy.start()
        for copy in fetches:
            copy.wait()
        body(*first, *near_in, *near_out, *rest)
        stores = [
            pltpu.make_async_copy(near, far, sems.at[n_in + i])
            for i, (near, far) in enumerate(zip(near_out, far_out))
        ]
        for copy in stores:
            copy.start()
        for copy in stores:
            copy.wait()

    hbm = pl.BlockSpec(memory_space=pltpu.HBM)
    return pl.pallas_call(
        kernel,
        out_shape=[jax.ShapeDtypeStruct(s, t) for s, t in outs],
        in_specs=[pl.BlockSpec(memory_space=pltpu.SMEM)] * scalars + [hbm] * n_in,
        out_specs=[hbm] * n_out,
        scratch_shapes=[pltpu.VMEM(a.shape, a.dtype) for a in arrays]
        + [pltpu.VMEM(s, t) for s, t in outs]
        + [pltpu.VMEM(*s) for s in scratch]
        + [pltpu.SemaphoreType.DMA((n_in + n_out,))],
        compiler_params=pltpu.CompilerParams(vmem_limit_bytes=VMEM_BYTES),
        cost_estimate=pl.CostEstimate(flops=flops, bytes_accessed=moved, transcendentals=exps),
    )(*args)


def swap_core(values):
    return lax.ppermute(values, "col", [(0, 1), (1, 0), (2, 3), (3, 2)])


def swap_chip(values):
    return lax.ppermute(values, "col", [(0, 2), (2, 0), (1, 3), (3, 1)])


def swap_half(values):
    return lax.ppermute(values, "row", [(i, i ^ 1) for i in range(lax.axis_size("row"))])


def sum_col(values):
    values = values + swap_core(values)
    return values + swap_chip(values)


def view_blocks(block):
    by_core = swap_core(block)
    by_chip = swap_chip(block)
    return (block, by_chip, by_core, swap_core(by_chip))


def token_pair(keep, send):
    pair = keep + swap_core(send).astype(jnp.float32)
    return (pair, swap_chip(pair.astype(jnp.bfloat16)))


def feature_sum(keep, send, beside=None):
    got = swap_core(send).astype(jnp.float32)
    far = swap_chip((keep[1] + got[1]).astype(jnp.bfloat16))
    if beside is not None:
        far, beside = lax.optimization_barrier((far, beside))
    total = keep[0] + got[0] + far.astype(jnp.float32)
    return total if beside is None else (total, beside)


def plane_exchange(values):
    rows = lax.axis_size("row")
    groups = [list(range(0, rows, 2)), list(range(1, rows, 2))]
    return lax.all_to_all(values, "row", 0, 0, axis_index_groups=groups, tiled=True)


def gather_pair(pair):
    count = lax.axis_size("row") // 2
    full = plane_exchange(jnp.broadcast_to(pair[None], (count,) + pair.shape))
    return full.reshape(-1, pair.shape[-1])


def sum_rows(grad, side):
    count = lax.axis_size("row") // 2
    height = grad.shape[0] // (2 * count)
    parts = plane_exchange(grad.reshape(count, 2 * height, -1))
    part = jnp.sum(parts.astype(jnp.float32), axis=0)
    low, high = part[:height], part[height:]
    got = swap_half(jnp.where(side == 0, high, low).astype(jnp.bfloat16))
    return jnp.where(side == 0, low, high) + got.astype(jnp.float32)


def per_device(
    hidden_in,
    segment_ids,
    cotangent,
    w_in,
    w_out,
    w_gate_up,
    w_down,
    norm_gains,
    ssm_gain,
    head_params,
    conv_weight,
    conv_bias,
):
    rows = lax.axis_size("row")
    column = lax.axis_index("col")
    side = lax.axis_index("row") % 2
    idx = jnp.stack([column // 2, column % 2]).astype(jnp.int32)
    shard = w_in.shape[1]
    in_cols = w_in.shape[2]
    bf16 = jnp.bfloat16
    f32 = jnp.float32
    length = hidden_in.shape[0]
    half = length // 2

    source = view_blocks(hidden_in)
    gains = view_blocks(norm_gains[0])
    pad_cols = -in_cols % 128
    wide = in_cols + pad_cols
    spread = jnp.broadcast_to(
        jnp.pad(w_in[0], ((0, 0), (0, pad_cols)))[None], (rows, shard, wide)
    )
    rest = jnp.concatenate([w_gate_up[0], w_down[0].T, w_out[0].T], 1)
    other = swap_half(rest)
    w_in_full = lax.all_to_all(spread, "row", 0, 0, tiled=True).reshape(rows * shard, wide)

    token128 = (length, 128)
    seg = segment_ids.astype(f32)[None, :]
    tok, cosine, sine, heads, skip = call(
        table_kernel,
        [(token128, f32)] * 3 + [((8, 128), f32), ((1, 384), f32)],
        seg, head_params[0],
    )
    gap = jnp.zeros((CONV, HEAD), f32)
    cweight = jnp.concatenate([conv_weight[0, :, :384], gap, conv_weight[0, :, 384:]], 1)
    cbias = jnp.concatenate([conv_bias[:, :384], gap[:1], conv_bias[:, 384:]], 1)
    chip0, core0 = idx[0] == 0, idx[1] == 0
    even = [jnp.where(core0, gains[i], gains[j]) for i, j in ((0, 2), (1, 3))]
    odd = [jnp.where(core0, gains[j], gains[i]) for i, j in ((0, 2), (1, 3))]
    gains = jnp.concatenate(
        [
            jnp.where(chip0, even[0], even[1]),
            jnp.where(chip0, odd[0], odd[1]),
            jnp.where(chip0, even[1], even[0]),
            jnp.where(chip0, odd[1], odd[0]),
        ],
        1,
    )

    rest = jnp.where(side == 0, jnp.stack([rest, other]), jnp.stack([other, rest]))
    tables = (w_in_full, rest, tok, seg, cosine, sine, heads, skip, cweight, cbias, gains)
    tables = lax.optimization_barrier(tables)
    w_in_full, rest, tok, seg, cosine, sine, heads, skip, cweight, cbias, gains = tables
    gain_a, gain_b = gains[0:1], gains[1:2]
    w_out_t = gather_pair(rest[:, :, 1536:])
    normed, scale_one, proj, xin, sent = call(
        in_kernel,
        [((length, D), bf16), ((length, 1), f32), ((length, wide), f32), ((length, 384), f32), (token128, bf16)],
        idx, *source, gain_a, w_in_full, cweight, cbias, tok,
        flops=2 * length * D * wide,
    )
    rest, sent = lax.optimization_barrier((rest, sent))
    w_mlp = gather_pair(rest[:, :, :1536])
    shared = view_blocks(sent)
    (
        attn, gated, ssm, ssq, probs, qrot, krot, value, state_b, state_c, step, cumc, cumr,
    ) = call(
        mixer_kernel,
        [(token128, bf16), ((length, 384), f32), ((length, 384), f32), ((8, length), f32), ((2, length, length), bf16)]
        + [(token128, bf16)] * 5
        + [(token128, f32)] * 2
        + [((8, length), f32)],
        idx, proj, xin, *shared, tok, seg, cosine, sine, heads, skip,
        flops=20 * length * length * 128,
        exps=8 * length * length,
    )
    ssq = sum_col(ssq)
    upstream = view_blocks(cotangent)
    mixed, scale_ssm, keep, send = call(
        mix_kernel,
        [((length, 512), bf16), ((length, 1), f32), ((half, D), f32), ((half, D), bf16)],
        idx, attn, gated, ssq, ssm_gain, w_out_t,
        flops=2 * length * 512 * D,
    )
    pair, got = token_pair(keep, send)
    after, scale_two, low = call(
        norm_kernel,
        [((half, D), f32), ((half, 1), f32), ((half, D), bf16)],
        idx, *source, pair, got, gain_b,
    )
    normed_two, up_one, act, grad_gu, keep, send = call(
        mlp_kernel,
        [((length, D), bf16)] * 2
        + [((length, 512), bf16), ((length, 1024), bf16), ((half, D), f32), ((half, D), bf16)],
        idx, low, swap_core(low), *upstream, w_mlp,
        flops=2 * length * D * 2560,
    )
    pair, got = token_pair(keep, send)
    (grads,) = call(
        grads_kernel, [((D, 1536), bf16)], up_one, act, normed_two, grad_gu,
        flops=2 * length * D * 1536,
    )
    got, grads = lax.optimization_barrier((got, grads))
    grads_mlp = sum_rows(grads, side)
    keep_down, send_down = call(
        down_kernel,
        [((2, length, 256), f32), ((2, length, 256), bf16)],
        idx, act, w_mlp, after,
        scratch=[((length, D), f32)],
        flops=2 * length * D * 512,
    )
    grad_mid, low, gain_two = call(
        norm_back_kernel,
        [((half, D), f32), ((half, D), bf16), ((1, D), f32)],
        idx, *upstream, pair, got, after, scale_two, gain_b,
    )
    up_two, grad_attn, scaled, inner, grad_ssm_gain = call(
        mix_back_kernel,
        [((length, D), bf16), (token128, f32), ((length, 384), f32), ((8, length), f32), ((1, 384), f32)],
        idx, low, swap_core(low), w_out_t, gated, scale_ssm, ssm_gain,
        flops=2 * length * D * 512,
    )
    inner, keep_down = lax.optimization_barrier((sum_col(inner), keep_down))
    hidden_out = feature_sum(keep_down, send_down).astype(bf16)
    dquery, dkey, dvalue = call(
        attention_back_kernel,
        [(token128, bf16), (token128, f32), (token128, f32)],
        grad_attn, attn, probs, qrot, krot, value, cosine, sine, tok,
        flops=12 * length * length * 128,
    )
    dproj, keep, send, small, conv_x = call(
        ssm_back_kernel,
        [((length, wide), bf16), ((2,) + token128, f32), ((2,) + token128, bf16), ((8, 128), f32), ((8, 384), f32)],
        idx, scaled, gated, ssm, scale_ssm, inner, dquery, proj, xin, step, cumc, cumr,
        state_b, state_c, tok, seg, heads, skip, cweight, cbias, dkey, dvalue,
        flops=30 * length * length * 128,
        exps=6 * length * length,
    )
    grad_sent = feature_sum(keep, send)
    grad_sent, grads_mlp = lax.optimization_barrier((grad_sent, grads_mlp))
    late, conv_s, gain_one, keep, send = call(
        in_back_kernel,
        [((length, wide), bf16), ((8, 128), f32), ((1, D), f32), ((2, length, 256), f32), ((2, length, 256), bf16)],
        idx, dproj, grad_sent, proj, tok, cweight, cbias, w_in_full, *source, scale_one, gain_a, grad_mid,
        scratch=[((length, D), f32)],
        flops=2 * length * D * wide,
    )
    gain_grads = sum_col(jnp.concatenate([gain_one, 0.5 * gain_two], 0))
    grad_hidden = feature_sum(keep, send)

    own = lax.dynamic_slice_in_dim(gain_grads, column * 256, 256, 1)
    grad_cweight = jnp.concatenate([conv_x[:CONV], conv_s[:CONV, HEAD:]], 1)
    grad_cbias = jnp.concatenate([conv_x[CONV], conv_s[CONV, HEAD:]])
    pieces = (own, grad_ssm_gain[0], small[:3, :6], grad_cweight, grad_cbias)
    flat = jnp.concatenate([piece.reshape(-1) for piece in pieces])
    flat = jnp.pad(flat, (0, shard * pad_cols - flat.shape[0])).astype(bf16)
    flat = jnp.pad(flat.reshape(shard, pad_cols), ((0, 0), (128 - pad_cols, 0)))
    (grads,) = call(
        last_grads_kernel, [((D, 512 + wide), bf16)], up_two, mixed, normed, late, flat,
        flops=2 * length * D * 1664,
    )
    total = sum_rows(grads, side)
    flat = total[:, 512 + in_cols :].reshape(-1)
    out_small = []
    start = 0
    for piece in pieces:
        out_small.append(flat[start : start + piece.size].reshape((1,) + piece.shape))
        start += piece.size
    return (
        hidden_out,
        grad_hidden,
        total[None, :, 512 : 512 + in_cols],
        total[:, :512].T[None],
        grads_mlp[None, :, 512:],
        grads_mlp[:, :512].T[None],
        *out_small,
    )


def solution(mesh):
    in_specs = (
        P("row", "col"),
        P("row"),
        P("row", "col"),
        P(None, "row", "col"),
        P(None, "col", "row"),
        P(None, "row", "col"),
        P(None, "col", "row"),
        P(None, None, "col"),
        P(None, "col"),
        P(None, None, "col"),
        P(None, None, "col"),
        P(None, "col"),
    )
    out_specs = (
        P("row", "col"),
        P("row", "col"),
        P(None, "row", "col"),
        P(None, "col", "row"),
        P(None, "row", "col"),
        P(None, "col", "row"),
        P(None, None, "col"),
        P(None, "col"),
        P(None, None, "col"),
        P(None, None, "col"),
        P(None, "col"),
    )
    return jax.shard_map(
        per_device, mesh=mesh, in_specs=in_specs, out_specs=out_specs, check_vma=False
    )
```

```python
import math

import jax
import jax.numpy as jnp
from jax import lax
from jax.experimental import pallas as pl
from jax.experimental.pallas import tpu as pltpu
from jax.sharding import PartitionSpec as P

D = 1024
Q_HEADS = 8
KV_HEADS = 2
HEAD = 64
SSM_HEADS = 24
SSM_HEAD = 64
STATE = 128
CONV = 4
FF = 2048
LAYERS = 1
CHUNK = 256
VMEM_BYTES = 60 * 1024 * 1024


epsilon = 1e-05
rope_base = 10000.0
contract_last = (((1,), (1,)), ((), ()))
contract_first = (((0,), (0,)), ((), ()))


def sequence_masks(segments):
    length = segments.shape[0]
    index = jnp.arange(length, dtype=jnp.int32)
    previous = jnp.concatenate([segments[:1], segments[:-1]])
    starts = jnp.where(segments != previous, index, 0)
    positions = (index - lax.cummax(starts, axis=0)).astype(jnp.float32)
    allowed = (segments[:, None] == segments[None, :]) & (index[:, None] >= index[None, :])
    shifted = []
    for shift in range(CONV):
        earlier = jnp.concatenate([jnp.full((shift,), -1, jnp.int32), segments[: length - shift]])
        shifted.append((earlier == segments).astype(jnp.float32))
    return (positions, allowed, jnp.stack(shifted))


def where_lane(shape, limit):
    return lax.broadcasted_iota(jnp.int32, shape, 1) < limit


def sigmoid(values):
    return 1.0 / (1.0 + jnp.exp(-values))


def softplus(values):
    return jnp.maximum(values, 0.0) + jnp.log1p(jnp.exp(-jnp.abs(values)))


def four_blocks(idx, own, by_chip, by_core, by_both):
    chip0 = idx[0] == 0
    core0 = idx[1] == 0
    first = jnp.where(chip0, own, by_chip)
    second = jnp.where(chip0, by_core, by_both)
    third = jnp.where(chip0, by_chip, own)
    fourth = jnp.where(chip0, by_both, by_core)
    return (
        jnp.where(core0, first, second),
        jnp.where(core0, second, first),
        jnp.where(core0, third, fourth),
        jnp.where(core0, fourth, third),
    )


def rotated(values, cosine, sine):
    lane = lax.broadcasted_iota(jnp.int32, values.shape, 1)
    other = jnp.where(lane % HEAD < HEAD // 2, pltpu.roll(values, 96, 1), pltpu.roll(values, 32, 1))
    return values * cosine + other * sine


def conv_pre(inner, weight, bias, valid):
    running = bias + weight[0:1] * inner * valid[:, 0:1]
    for shift in range(1, CONV):
        running = running + weight[shift : shift + 1] * pltpu.roll(inner, shift, 0) * valid[
            :, shift : shift + 1
        ]
    return running


def conv_back(grad, inner, weight, valid):
    length = inner.shape[0]
    total = weight[0:1] * (grad * valid[:, 0:1])
    taps = [jnp.sum(grad * valid[:, 0:1] * inner, axis=0, keepdims=True)]
    for shift in range(1, CONV):
        seen = grad * valid[:, shift : shift + 1]
        total = total + weight[shift : shift + 1] * pltpu.roll(seen, length - shift, 0)
        taps.append(jnp.sum(seen * pltpu.roll(inner, shift, 0), axis=0, keepdims=True))
    return (total, taps, jnp.sum(grad, axis=0, keepdims=True))


def silu_slope(values, sig):
    return sig * (1.0 + values * (1.0 - sig))


def dot32(left, right, dims=(((1,), (0,)), ((), ()))):
    return lax.dot_general(left, right, dims, preferred_element_type=jnp.float32)


def exact(left, right):
    return lax.dot_general(
        left,
        right,
        (((1,), (0,)), ((), ())),
        precision=lax.Precision.HIGHEST,
        preferred_element_type=jnp.float32,
    )


def triangle(length, reverse=False):
    first = lax.broadcasted_iota(jnp.int32, (length, length), 0)
    second = lax.broadcasted_iota(jnp.int32, (length, length), 1)
    return jnp.where(second >= first if reverse else first >= second, 1.0, 0.0)


def head_sums(width):
    lane = lax.broadcasted_iota(jnp.int32, (width, 128), 0) // SSM_HEAD
    head = lax.broadcasted_iota(jnp.int32, (width, 128), 1)
    return jnp.where(lane == head, 1.0, 0.0)


def per_head(columns, tile, shape):
    return jnp.where(
        where_lane(shape, SSM_HEAD),
        jnp.broadcast_to(columns[:, 2 * tile : 2 * tile + 1], shape),
        jnp.broadcast_to(columns[:, 2 * tile + 1 : 2 * tile + 2], shape),
    )


def chunk_allowed(tok, seg, start, count):
    rows = tok.shape[0]
    time = lax.broadcasted_iota(jnp.int32, (rows, count), 0) + start
    source = lax.broadcasted_iota(jnp.int32, (rows, count), 1)
    return (tok[:, 4:5] == seg[0:1, :count]) & (time >= source)


def table_kernel(seg, params, tok_out, cosine_out, sine_out, heads_out, skip_out):
    length = seg.shape[1]
    shape = (length, 128)
    column = row_to_column(seg[...])
    time = lax.broadcasted_iota(jnp.int32, (length, 1), 0)
    allowed = chunk_allowed(jnp.broadcast_to(column, (length, 8)), seg[...], 0, length)
    positions = jnp.sum(jnp.where(allowed, 1.0, 0.0), axis=1, keepdims=True) - 1.0
    lane = lax.broadcasted_iota(jnp.int32, shape, 1)
    wide = jnp.broadcast_to(column, shape)
    tok = jnp.where(lane == 4, wide, 0.0)
    for shift in range(CONV):
        same = wide == (pltpu.roll(wide, shift, 0) if shift else wide)
        tok = jnp.where((lane == shift) & same & (time >= shift), 1.0, tok)
    tok_out[...] = tok
    slot = (lane % (HEAD // 2)).astype(jnp.float32)
    angle = positions * jnp.exp(slot * (-2.0 * math.log(rope_base) / HEAD))
    cosine_out[...] = jnp.cos(angle)
    sine = jnp.sin(angle)
    sine_out[...] = jnp.where(lane % HEAD < HEAD // 2, -sine, sine)
    heads_out[...] = jnp.zeros(heads_out.shape, jnp.float32)
    heads_out[0:3, 0:6] = params[...]
    lane = lax.broadcasted_iota(jnp.int32, skip_out.shape, 1) // SSM_HEAD
    skip = jnp.zeros(skip_out.shape, jnp.float32)
    for head in range(params.shape[1]):
        skip = jnp.where(lane == head, params[1:2, head : head + 1], skip)
    skip_out[...] = skip


def in_kernel(
    idx, own, by_chip, by_core, by_both, gain, weight, cweight, cbias, tok,
    normed_out, scale_out, inner_out, tile_out, raw_out, xin_out, sent_out,
):
    source = jnp.concatenate(
        four_blocks(idx, own[...], by_chip[...], by_core[...], by_both[...]), 1
    ).astype(jnp.float32)
    scale = lax.rsqrt(jnp.sum(source * source, axis=1, keepdims=True) / D + epsilon)
    normed = (source * scale * gain[0:1]).astype(jnp.bfloat16)
    normed_out[...] = normed
    normed_out.send()
    scale_out[...] = scale
    proj = dot32(normed, weight[...])
    inner = proj[:, :512]
    inner_out[...] = proj[:, :384]
    tile_out[...] = proj[:, 384:512]
    raw_out[...] = proj[:, 512:]
    pre = conv_pre(inner, cweight[...], cbias[0:1], tok[...])
    active = pre * sigmoid(pre)
    tile = inner[:, 384:]
    sent_out[...] = jnp.where(where_lane(tile.shape, HEAD), tile, active[:, 384:]).astype(
        jnp.bfloat16
    )
    xin_out[...] = active[:, :384]


def mixer_kernel(
    idx, normed, weight, raw, xin, own, by_chip, by_core, by_both, tok, seg, cosine, sine, heads,
    skip, gain,
    attn_out, gate_out, gated_out, ssm_out, ssq_out, probs_out, qrot_out, krot_out, value_out,
    state_b_out, state_c_out, step_out, cumc_out, cumr_out, keep_out, send_out, scaled,
):
    f32 = jnp.float32
    bf16 = jnp.bfloat16
    length = normed.shape[0]
    proj = dot32(normed[...], weight[:, :512])
    gate_out[...] = proj[:, 128:]
    gate_out.send()
    blocks = four_blocks(
        idx, own[...].astype(f32), by_chip[...].astype(f32), by_core[...].astype(f32),
        by_both[...].astype(f32),
    )
    chip0 = idx[0] == 0
    shape = (length, 128)
    left = where_lane(shape, HEAD)
    keys = jnp.where(chip0, blocks[0], blocks[1])
    values = jnp.where(chip0, blocks[2], blocks[3])
    keys = jnp.where(left, keys, pltpu.roll(keys, 64, 1))
    values = jnp.where(left, values, pltpu.roll(values, 64, 1)).astype(bf16)
    state_b = jnp.where(left, pltpu.roll(blocks[0], 64, 1), blocks[1]).astype(bf16)
    state_c = jnp.where(left, pltpu.roll(blocks[2], 64, 1), blocks[3]).astype(bf16)
    krot = rotated(keys, cosine[...], sine[...]).astype(bf16)
    qrot = rotated(proj[:, :128], cosine[...], sine[...]).astype(bf16)
    value_out[...] = values
    state_b_out[...] = state_b
    state_c_out[...] = state_c
    krot_out[...] = krot
    qrot_out[...] = qrot
    step = softplus(raw[...] + heads[2:3])
    step_out[...] = step
    cum = exact(triangle(length), step * -jnp.exp(heads[0:1]))
    cumc_out[...] = cum
    cumr = cum.T[:8]
    cumr_out[...] = cumr
    xin_all = xin[...]
    tiles = xin_all.shape[1] // 128
    inputs = [
        (per_head(step, tile, shape) * xin_all[:, 128 * tile : 128 * tile + 128]).astype(bf16)
        for tile in range(tiles)
    ]
    half = min(CHUNK, length)
    for start in range(0, length, half):
        count = start + half
        rows = slice(start, count)
        allowed = chunk_allowed(tok[rows, :], seg[...], start, count)
        first = where_lane((half, 128), HEAD)
        outs = []
        for head in range(2):
            query = jnp.where(first == (head == 0), qrot[rows].astype(f32), 0.0).astype(bf16)
            scores = dot32(query, krot[:count], contract_last) * HEAD ** (-0.5)
            scores = jnp.where(allowed, scores, -1e30)
            weights = jnp.exp(scores - jnp.max(scores, axis=1, keepdims=True))
            probs = (weights / jnp.sum(weights, axis=1, keepdims=True)).astype(bf16)
            probs_out[head, rows, :count] = probs
            outs.append(dot32(probs, values[:count]))
        attn_out[rows, :] = jnp.where(first, outs[0], outs[1]).astype(bf16)
        gram = dot32(state_c[rows], state_b[:count], contract_last)
        total = jnp.zeros((half, 128), f32)
        for tile in range(tiles):
            lanes = slice(128 * tile, 128 * tile + 128)
            outs = []
            for head in (2 * tile, 2 * tile + 1):
                diff = cum[rows, head : head + 1] - cumr[head : head + 1, :count]
                mixing = jnp.exp(jnp.where(allowed, diff, -1e30)) * gram
                outs.append(dot32(mixing.astype(bf16), inputs[tile][:count]))
            ssm = jnp.where(first, outs[0], outs[1]) + skip[0:1, lanes] * xin_all[rows, lanes]
            ssm_out[rows, lanes] = ssm
            gate = proj[rows, 128 + 128 * tile : 256 + 128 * tile]
            gated = ssm * (gate * sigmoid(gate))
            gated_out[rows, lanes] = gated
            scaled[rows, lanes] = (gated * gain[0:1, lanes]).astype(bf16)
            total = total + gated * gated
        ssq_out[:, rows] = lax.dot_general(
            jnp.ones((8, 128), f32),
            total,
            contract_last,
            precision=lax.Precision.HIGHEST,
            preferred_element_type=f32,
        )
    core = idx[1]
    for place, rows in ((0, half_rows(1 - core, length)), (1, half_rows(core, length))):
        for part, left, lanes in ((0, attn_out, (512, 640)), (1, scaled, (640, 1024))):
            product = dot32(left[rows, :], weight[:, lanes[0] : lanes[1]], contract_last)
            if place == 0:
                send_out[part, :, :] = product.astype(bf16)
            else:
                keep_out[part, :, :] = product
        if place == 0:
            send_out.send()


def attention_back_kernel(
    grad, attn, probs, qrot, krot, value, cosine, sine, tok,
    dquery_out, dkey_out, dvalue_out,
):
    f32 = jnp.float32
    bf16 = jnp.bfloat16
    length = grad.shape[0]
    shape = (length, 128)
    lane0 = where_lane(shape, HEAD)
    dkey = [jnp.zeros(shape, f32), jnp.zeros(shape, f32)]
    dvalue = jnp.zeros(shape, f32)
    half = min(CHUNK, length)
    dquery = []
    keyparts = []
    valueparts = []
    for start in range(0, length, half):
        count = start + half
        rows = slice(start, count)
        first = where_lane((half, 128), HEAD)
        dout = grad[rows, :]
        product = dout * attn[rows, :].astype(f32)
        outs = []
        dk = []
        dv = []
        for head in range(2):
            mine = first == (head == 0)
            dhead = jnp.where(mine, dout, 0.0).astype(bf16)
            query = jnp.where(mine, qrot[rows, :].astype(f32), 0.0).astype(bf16)
            part = probs[head, rows, :count]
            dprob = dot32(dhead, value[:count, :], contract_last)
            inner = jnp.sum(jnp.where(mine, product, 0.0), axis=1, keepdims=True)
            dscore = (part.astype(f32) * (dprob - inner) * HEAD ** (-0.5)).astype(bf16)
            outs.append(dot32(dscore, krot[:count, :]))
            dk.append(dot32(dscore, query, contract_first))
            dv.append(dot32(part, dhead, contract_first))
        dquery.append(jnp.where(first, outs[0], outs[1]))
        keyparts.append(dk[0] + dk[1])
        valueparts.append(dv[0] + dv[1])

    def gathered(parts):
        total = parts[-1]
        for part in parts[:-1]:
            pad = jnp.zeros((length - part.shape[0], 128), f32)
            total = total + jnp.concatenate([part, pad], 0)
        return total + pltpu.roll(total, 64, 1)

    back = -sine[...]
    dquery_out[...] = rotated(jnp.concatenate(dquery, 0), cosine[...], back).astype(bf16)
    dkey_out[...] = rotated(gathered(keyparts), cosine[...], back)
    dvalue_out[...] = gathered(valueparts)


def ssm_back_kernel(
    idx, scaled, gated, ssm, scale_ssm, inner, dquery, gates, inners, raw, xin, step, cumc, cumr, state_b, state_c,
    tok, seg, heads, skip, cweight, cbias, dkey, dvalue,
    dproj_out, dstep_out, keep_out, send_out, small_out, conv_out,
):
    f32 = jnp.float32
    bf16 = jnp.bfloat16
    length = xin.shape[0]
    shape = (length, 128)
    tiles = xin.shape[1] // 128
    scale = scale_ssm[...]
    shrink = scale * scale * scale * row_to_column(inner[...]) / (SSM_HEADS * SSM_HEAD)
    dproj_out[:, :128] = dquery[...]
    step_all = step[...]
    left = where_lane(shape, HEAD)
    grads = []
    grads_low = []
    inputs = []
    for tile in range(tiles):
        lanes = slice(128 * tile, 128 * tile + 128)
        gate = gates[:, lanes]
        sig = sigmoid(gate)
        grad_gated = scale * scaled[:, lanes] - gated[:, lanes] * shrink
        dproj_out[:, 128 + 128 * tile : 256 + 128 * tile] = (grad_gated * ssm[:, lanes] * silu_slope(gate, sig)).astype(bf16)
        grad = grad_gated * gate * sig
        grads.append(grad)
        grads_low.append(grad.astype(bf16))
        inputs.append((per_head(step_all, tile, shape) * xin[:, lanes]).astype(bf16))
    half = min(CHUNK, length)
    dinputs = [[] for _ in range(tiles)]
    dstate_b = []
    dstate_c = []
    for start in range(0, length, half):
        count = start + half
        rows = slice(start, count)
        allowed = chunk_allowed(tok[rows, :], seg[...], start, count)
        first = where_lane((half, 128), HEAD)
        gram = dot32(state_c[rows, :], state_b[:count, :], contract_last)
        dgram = jnp.zeros((half, count), f32)
        for tile in range(tiles):
            pair = []
            low = grads_low[tile][rows]
            for head in (2 * tile, 2 * tile + 1):
                diff = cumc[rows, head : head + 1] - cumr[head : head + 1, :count]
                decay = jnp.exp(jnp.where(allowed, diff, -1e30))
                mixing = (decay * gram).astype(bf16)
                mine = jnp.where(first == (head % 2 == 0), low.astype(f32), 0.0).astype(bf16)
                dgram = dgram + decay * dot32(mine, inputs[tile][:count], contract_last)
                pair.append(dot32(mixing, low, contract_first))
            dinputs[tile].append(jnp.where(where_lane((count, 128), HEAD), pair[0], pair[1]))
        dgram = dgram.astype(bf16)
        dstate_c.append(dot32(dgram, state_b[:count, :]))
        dstate_b.append(dot32(dgram, state_c[rows, :], contract_first))

    def gathered(parts):
        total = parts[-1]
        for part in parts[:-1]:
            pad = jnp.zeros((length - part.shape[0], 128), f32)
            total = total + jnp.concatenate([part, pad], 0)
        return total

    valid = tok[...]
    balance = jnp.zeros(shape, f32)
    dstep = jnp.zeros(shape, f32)
    dskip = jnp.zeros((1, 128), f32)
    sums = head_sums(128 * tiles)
    for tile in range(tiles):
        lanes = slice(128 * tile, 128 * tile + 128)
        dinput = gathered(dinputs[tile])
        own = xin[:, lanes]
        plain = ssm[:, lanes] - skip[0:1, lanes] * own
        select = sums[128 * tile : 128 * tile + 128]
        balance = balance + exact(
            grads_low[tile].astype(f32) * plain - inputs[tile].astype(f32) * dinput, select
        )
        dstep = dstep + exact(dinput * own, select)
        dskip = dskip + exact(
            jnp.broadcast_to(jnp.sum(grads[tile] * own, axis=0, keepdims=True), (8, 128)), select
        )[0:1]
        dxin = skip[0:1, lanes] * grads[tile] + per_head(step_all, tile, shape) * dinput
        source = inners[:, lanes]
        weight = cweight[:, lanes]
        pre = conv_pre(source, weight, cbias[0:1, lanes], valid)
        dpre = dxin * silu_slope(pre, sigmoid(pre))
        dsource, taps, dbias = conv_back(dpre, source, weight, valid)
        dproj_out[:, 512 + 128 * tile : 640 + 128 * tile] = dsource.astype(bf16)
        for shift in range(CONV):
            conv_out[shift : shift + 1, lanes] = taps[shift]
        conv_out[CONV : CONV + 1, lanes] = dbias
    rate = -jnp.exp(heads[0:1])
    dlog = exact(triangle(length, True), balance)
    dstep = (dstep + dlog * rate) * sigmoid(raw[...] + heads[2:3])
    dstep = jnp.where(where_lane(shape, SSM_HEADS // 4), dstep, 0.0)
    dstep_out[...] = dstep.astype(bf16)
    small_out[0:1, :] = jnp.sum(dlog * step_all, axis=0, keepdims=True) * rate
    small_out[1:2, :] = dskip
    small_out[2:3, :] = jnp.sum(dstep, axis=0, keepdims=True)
    small_out[3:8, :] = jnp.zeros((5, 128), f32)
    dstate_b = gathered(dstate_b)
    dstate_c = jnp.concatenate(dstate_c, 0)
    chip0 = idx[0] == 0
    core0 = idx[1] == 0
    none = jnp.zeros(shape, f32)
    dkey0 = jnp.where(chip0, dkey[...], none)
    dkey1 = jnp.where(chip0, none, dkey[...])
    dvalue0 = jnp.where(chip0, dvalue[...], none)
    dvalue1 = jnp.where(chip0, none, dvalue[...])
    pieces = (
        jnp.where(left, dkey0, pltpu.roll(dstate_b, 64, 1)),
        jnp.where(left, dkey1, dstate_b),
        jnp.where(left, dvalue0, pltpu.roll(dstate_c, 64, 1)),
        jnp.where(left, dvalue1, dstate_c),
    )
    near = (jnp.where(core0, pieces[0], pieces[1]), jnp.where(core0, pieces[2], pieces[3]))
    away = (jnp.where(core0, pieces[1], pieces[0]), jnp.where(core0, pieces[3], pieces[2]))
    keep_out[0, :, :] = jnp.where(chip0, near[0], near[1])
    keep_out[1, :, :] = jnp.where(chip0, near[1], near[0])
    send_out[0, :, :] = jnp.where(chip0, away[0], away[1]).astype(bf16)
    send_out[1, :, :] = jnp.where(chip0, away[1], away[0]).astype(bf16)


def row_to_column(row):
    return jnp.broadcast_to(row[0:1], (128, row.shape[1])).T[:, 0:1]


def half_rows(core, length):
    return pl.ds(pl.multiple_of(core * (length // 2), length // 2), length // 2)


def block_halves(idx, blocks):
    rows = half_rows(idx[1], blocks[0].shape[0])
    return jnp.concatenate(four_blocks(idx, *(block[rows, :] for block in blocks)), 1).astype(
        jnp.float32
    )


def norm_kernel(idx, own, by_chip, by_core, by_both, pair, got, gain, after_out, scale_out, low_out):
    after = (
        block_halves(idx, (own, by_chip, by_core, by_both))
        + pair[...]
        + got[...].astype(jnp.float32)
    )
    scale = lax.rsqrt(jnp.sum(after * after, axis=1, keepdims=True) / D + epsilon)
    after_out[...] = after
    scale_out[...] = scale
    low_out[...] = (after * scale * gain[0:1]).astype(jnp.bfloat16)


def joined(idx, near, away):
    core0 = idx[1] == 0
    near, away = near[...], away[...]
    return jnp.concatenate([jnp.where(core0, near, away), jnp.where(core0, away, near)], 0)


def mlp_kernel(
    idx, near, away, own, by_chip, by_core, by_both, weights,
    normed_out, up_out, act_out, grad_out, keep_out, send_out,
):
    length = own.shape[0]
    cols = weights.shape[1] // 3
    normed = joined(idx, near, away)
    normed_out[...] = normed
    normed_out.send()
    upstream = jnp.concatenate(
        four_blocks(idx, own[...], by_chip[...], by_core[...], by_both[...]), 1
    )
    up_out[...] = upstream
    up_out.send()
    both = dot32(normed, weights[:, : 2 * cols])
    gate = both[:, :cols]
    upper = both[:, cols:]
    sig = sigmoid(gate)
    act_out[...] = (gate * sig * upper).astype(jnp.bfloat16)
    grad = dot32(upstream, weights[:, 2 * cols :])
    grad_out[:, :cols] = (grad * upper * silu_slope(gate, sig)).astype(jnp.bfloat16)
    grad_out[:, cols:] = (grad * gate * sig).astype(jnp.bfloat16)
    core = idx[1]
    away = grad_out[half_rows(1 - core, length), :]
    send_out[...] = dot32(away, weights[:, : 2 * cols], contract_last).astype(jnp.bfloat16)
    send_out.send()
    keep_out[...] = dot32(
        grad_out[half_rows(core, length), :], weights[:, : 2 * cols], contract_last
    )


def norm_back_kernel(
    idx, own, by_chip, by_core, by_both, pair, got, after, scale, gain, grad_out, low_out, gain_out
):
    partial = pair[...] + got[...].astype(jnp.float32)
    source = after[...]
    r = scale[...]
    scaled = partial * gain[0:1]
    inner = jnp.sum(scaled * source, axis=1, keepdims=True)
    grad = (
        block_halves(idx, (own, by_chip, by_core, by_both))
        + r * scaled
        - source * (r * r * r * inner / D)
    )
    grad_out[...] = grad
    low_out[...] = grad.astype(jnp.bfloat16)
    gain_out[...] = jnp.sum(partial * source * r, axis=0, keepdims=True)


def mix_back_kernel(
    idx, near, away, weight, attn, gated, total, gain,
    up_out, attn_out, scaled_out, inner_out, gain_out, scale_out, mixed_out,
):
    upstream = joined(idx, near, away)
    up_out[...] = upstream
    up_out.send()
    grad = dot32(upstream, weight[:, 512:])
    attn_out[...] = grad[:, :128]
    grad = grad[:, 128:]
    scaled = grad * gain[0:1]
    scaled_out[...] = scaled
    source = gated[...]
    scale = lax.rsqrt(row_to_column(total[...]) / (SSM_HEADS * SSM_HEAD) + epsilon)
    scale_out[...] = scale
    product = scaled * source
    inner_out[...] = lax.dot_general(
        jnp.ones((8, product.shape[1]), jnp.float32),
        product,
        contract_last,
        precision=lax.Precision.HIGHEST,
        preferred_element_type=jnp.float32,
    )
    normal = source * scale
    gain_out[...] = jnp.sum(grad * normal, axis=0, keepdims=True)
    mixed_out[:, :128] = attn[...]
    mixed_out[:, 128:] = (normal * gain[0:1]).astype(jnp.bfloat16)


def feature_blocks(idx, total, keep_out, send_out):
    chip, core = idx[0], idx[1]
    for place, way in ((0, chip), (1, 1 - chip)):
        near = pl.multiple_of((2 * way + core) * 256, 256)
        away = pl.multiple_of((2 * way + 1 - core) * 256, 256)
        keep_out[place, :, :] = total[:, pl.ds(near, 256)]
        send_out[place, :, :] = total[:, pl.ds(away, 256)].astype(jnp.bfloat16)


def add_residual(idx, total, resid):
    rows = half_rows(idx[1], total.shape[0])
    lanes = pl.ds(pl.multiple_of(idx[0] * (D // 2), D // 2), D // 2)
    total[rows, lanes] = total[rows, lanes] + resid[:, lanes]


def down_kernel(idx, act, weight, resid, keep_out, send_out, total):
    total[...] = dot32(act[...], weight[:, 1024:], contract_last)
    add_residual(idx, total, resid)
    feature_blocks(idx, total, keep_out, send_out)


def in_back_kernel(
    idx, dproj, dstep, dsent, tile_in, tok, cweight, cbias, weight_qz, weight_rest,
    own, by_chip, by_core, by_both, scale, gain, grad_mid,
    late_out, conv_out, gain_out, keep_out, send_out, total,
):
    inner = tile_in[...]
    taps_in = cweight[:, 384:]
    valid = tok[...]
    pre = conv_pre(inner, taps_in, cbias[0:1, 384:], valid)
    grad = dsent[...]
    dpre = grad * silu_slope(pre, sigmoid(pre))
    dinner, taps, dbias = conv_back(dpre, inner, taps_in, valid)
    for shift in range(CONV):
        conv_out[shift : shift + 1, :] = taps[shift]
    conv_out[CONV : CONV + 1, :] = dbias
    conv_out[CONV + 1 :, :] = jnp.zeros((7 - CONV, 128), jnp.float32)
    tile = jnp.where(where_lane(grad.shape, HEAD), grad, dinner).astype(jnp.bfloat16)
    late = jnp.concatenate([tile, dstep[...]], 1)
    late_out[...] = late
    partial = dot32(dproj[:, :512], weight_qz[:, :512], contract_last) + dot32(
        jnp.concatenate([dproj[:, 512:], late], 1), weight_rest[...], contract_last
    )
    source = jnp.concatenate(
        four_blocks(idx, own[...], by_chip[...], by_core[...], by_both[...]), 1
    ).astype(jnp.float32)
    r = scale[...]
    scaled = partial * gain[0:1]
    dots = jnp.sum(scaled * source, axis=1, keepdims=True)
    total[...] = r * scaled - source * (r * r * r * dots / D)
    gain_out[...] = jnp.sum(partial * source * r, axis=0, keepdims=True)
    add_residual(idx, total, grad_mid)
    feature_blocks(idx, total, keep_out, send_out)


def grads_kernel(first, second, third, fourth, out):
    cols = second.shape[1]
    more = out.shape[1] - cols
    out[:, :cols] = dot32(first[...], second[...], contract_first).astype(jnp.bfloat16)
    out[:, cols:] = dot32(third[...], fourth[:, :more], contract_first).astype(jnp.bfloat16)


def late_grads_kernel(normed, dproj, late, small, out):
    right = jnp.concatenate([dproj[:, 512:], late[...]], 1)
    out[...] = dot32(normed[...], right, contract_first).astype(jnp.bfloat16)
    shard = small.shape[0]
    first = where_lane((shard, 128), 6)
    for start in range(0, out.shape[0], shard):
        rows = slice(start, start + shard)
        out[rows, 512:] = jnp.where(
            first, out[rows, 512:].astype(jnp.float32), small[...].astype(jnp.float32)
        ).astype(jnp.bfloat16)


class Fetch:
    def __init__(self, copy, ref):
        self.copy, self.ref, self.shape, self.open = copy, ref, ref.shape, True
        copy.start()

    def wait(self):
        if self.open:
            self.open = False
            self.copy.wait()

    def __getitem__(self, at):
        self.wait()
        return self.ref[at]


class Store:
    def __init__(self, copy, ref):
        self.copy, self.ref, self.shape, self.open = copy, ref, ref.shape, True

    def __setitem__(self, at, value):
        self.ref[at] = value

    def __getitem__(self, at):
        return self.ref[at]

    def send(self):
        if self.open:
            self.open = False
            self.copy.start()


def call(body, outs, *args, scratch=(), us=1.0):
    scalars = sum(a.dtype == jnp.int32 for a in args)
    arrays = args[scalars:]
    n_in, n_out = len(arrays), len(outs)

    def kernel(*refs):
        first = refs[:scalars]
        refs = refs[scalars:]
        far_in, far_out = refs[:n_in], refs[n_in : n_in + n_out]
        refs = refs[n_in + n_out :]
        near_in, near_out = refs[:n_in], refs[n_in : n_in + n_out]
        *rest, sems = refs[n_in + n_out :]
        fetches = [
            Fetch(pltpu.make_async_copy(far, near, sems.at[i]), near)
            for i, (far, near) in enumerate(zip(far_in, near_in))
        ]
        stores = [
            Store(pltpu.make_async_copy(near, far, sems.at[n_in + i]), near)
            for i, (near, far) in enumerate(zip(near_out, far_out))
        ]
        body(*first, *fetches, *stores, *rest)
        for item in fetches:
            item.wait()
        for item in stores:
            item.send()
        for item in stores:
            item.copy.wait()

    hbm = pl.BlockSpec(memory_space=pltpu.HBM)
    return pl.pallas_call(
        kernel,
        out_shape=[jax.ShapeDtypeStruct(s, t) for s, t in outs],
        in_specs=[pl.BlockSpec(memory_space=pltpu.SMEM)] * scalars + [hbm] * n_in,
        out_specs=[hbm] * n_out,
        scratch_shapes=[pltpu.VMEM(a.shape, a.dtype) for a in arrays]
        + [pltpu.VMEM(s, t) for s, t in outs]
        + [pltpu.VMEM(*s) for s in scratch]
        + [pltpu.SemaphoreType.DMA((n_in + n_out,))],
        compiler_params=pltpu.CompilerParams(vmem_limit_bytes=VMEM_BYTES),
        cost_estimate=pl.CostEstimate(
            flops=int(us * 1.15e9), bytes_accessed=int(us * 3.69e6), transcendentals=0
        ),
    )(*args)


def swap_core(values):
    return lax.ppermute(values, "col", [(0, 1), (1, 0), (2, 3), (3, 2)])


def swap_chip(values):
    return lax.ppermute(values, "col", [(0, 2), (2, 0), (1, 3), (3, 1)])


def swap_both(values):
    return lax.ppermute(values, "col", [(0, 3), (3, 0), (1, 2), (2, 1)])


def swap_half(values):
    return lax.ppermute(values, "row", [(i, i ^ 1) for i in range(lax.axis_size("row"))])


def sum_col(values):
    values = values + swap_core(values)
    return values + swap_chip(values)


def view_blocks(block):
    by_core = swap_core(block)
    by_chip = swap_chip(block)
    return (block, by_chip, by_core, swap_core(by_chip))


def token_pair(keep, send, after):
    pair = keep + swap_core(send).astype(jnp.float32)
    low, after = lax.optimization_barrier((pair.astype(jnp.bfloat16), after))
    return (pair, swap_chip(low), after)


def feature_sum(keep, send, after=None):
    got = swap_core(send)
    low = (keep[1] + got[1].astype(jnp.float32)).astype(jnp.bfloat16)
    if after is not None:
        low, after = lax.optimization_barrier((low, after))
    total = keep[0] + got[0].astype(jnp.float32) + swap_chip(low).astype(jnp.float32)
    return total if after is None else (total, after)


def plane_exchange(values):
    rows = lax.axis_size("row")
    groups = [list(range(0, rows, 2)), list(range(1, rows, 2))]
    return lax.all_to_all(values, "row", 0, 0, axis_index_groups=groups, tiled=True)


def gather_pair(pair):
    count = lax.axis_size("row") // 2
    full = plane_exchange(jnp.broadcast_to(pair[None], (count,) + pair.shape))
    return full.reshape(-1, pair.shape[-1])


def send_rows(grad):
    count = lax.axis_size("row") // 2
    return plane_exchange(grad.reshape(count, grad.shape[0] // count, -1))


def sum_rows(parts, side):
    height = parts.shape[1] // 2
    part = jnp.sum(parts.astype(jnp.float32), axis=0)
    low, high = part[:height], part[height:]
    got = swap_half(jnp.where(side == 0, high, low).astype(jnp.bfloat16))
    return jnp.where(side == 0, low, high) + got.astype(jnp.float32)


def per_device(
    hidden_in,
    segment_ids,
    cotangent,
    w_in,
    w_out,
    w_gate_up,
    w_down,
    norm_gains,
    ssm_gain,
    head_params,
    conv_weight,
    conv_bias,
):
    rows = lax.axis_size("row")
    column = lax.axis_index("col")
    side = lax.axis_index("row") % 2
    idx = jnp.stack([column // 2, column % 2]).astype(jnp.int32)
    shard = w_in.shape[1]
    in_cols = w_in.shape[2]
    bf16 = jnp.bfloat16
    f32 = jnp.float32
    length = hidden_in.shape[0]
    half = length // 2

    source = view_blocks(hidden_in)
    gains = view_blocks(norm_gains[0])
    early_cols = 512
    pad_cols = -in_cols % 128
    first = jnp.pad(w_in[0, :, early_cols:], ((0, 0), (0, pad_cols)))
    rest = jnp.concatenate([w_in[0, :, :early_cols], w_out[0].T, w_gate_up[0], w_down[0].T], 1)
    other = swap_half(rest)
    spread = jnp.broadcast_to(first[None], (rows,) + first.shape)
    weight_rest = lax.all_to_all(spread, "row", 0, 0, tiled=True).reshape(D, -1)

    token128 = (length, 128)
    seg = segment_ids.astype(f32)[None, :]
    tok, cosine, sine, heads, skip = call(
        table_kernel,
        [(token128, f32)] * 3 + [((8, 128), f32), ((1, 384), f32)],
        seg, head_params[0],
        us=2,
    )
    gap = jnp.zeros((CONV, HEAD), f32)
    cweight = jnp.concatenate([conv_weight[0, :, :384], gap, conv_weight[0, :, 384:]], 1)
    cbias = jnp.concatenate([conv_bias[:, :384], gap[:1], conv_bias[:, 384:]], 1)
    chip0, core0 = idx[0] == 0, idx[1] == 0
    even = [jnp.where(core0, gains[i], gains[j]) for i, j in ((0, 2), (1, 3))]
    odd = [jnp.where(core0, gains[j], gains[i]) for i, j in ((0, 2), (1, 3))]
    gains = jnp.concatenate(
        [
            jnp.where(chip0, even[0], even[1]),
            jnp.where(chip0, odd[0], odd[1]),
            jnp.where(chip0, even[1], even[0]),
            jnp.where(chip0, odd[1], odd[0]),
        ],
        1,
    )

    rest = jnp.where(side == 0, jnp.stack([rest, other]), jnp.stack([other, rest]))
    tables = (
        weight_rest, rest, tok, seg, cosine, sine, heads, skip, cweight, cbias, gains, *source
    )
    tables = lax.optimization_barrier(tables)
    weight_rest, rest, tok, seg, cosine, sine, heads, skip, cweight, cbias, gains, *source = tables
    gain_a, gain_b = gains[0:1], gains[1:2]
    weight_mix = gather_pair(rest[:, :, :1024])
    normed, scale_one, inners, tile_in, raw, xin, sent = call(
        in_kernel,
        [((length, D), bf16), ((length, 1), f32), ((length, 384), f32), (token128, f32), (token128, f32)]
        + [((length, 384), f32), (token128, bf16)],
        idx, *source, gain_a, weight_rest, cweight, cbias, tok,
        us=5.4,
    )
    shared = view_blocks(sent)
    rest, weight_mix, *shared = lax.optimization_barrier((rest, weight_mix, *shared))
    w_mlp = gather_pair(rest[:, :, 1024:])
    (
        attn, gates, gated, ssm, ssq, probs, qrot, krot, value, state_b, state_c, step, cumc, cumr,
        keep, send,
    ) = call(
        mixer_kernel,
        [(token128, bf16)]
        + [((length, 384), f32)] * 3
        + [((8, length), f32), ((2, length, length), bf16)]
        + [(token128, bf16)] * 5
        + [(token128, f32)] * 2
        + [((8, length), f32), ((2, half, D), f32), ((2, half, D), bf16)],
        idx, normed, weight_mix, raw, xin, *shared, tok, seg, cosine, sine, heads, skip, ssm_gain,
        scratch=[((length, 384), bf16)],
        us=14.4,
    )
    ssq = sum_col(ssq)
    ratio = lax.rsqrt(ssq[0] / (SSM_HEADS * SSM_HEAD) + epsilon)
    ratio = jnp.where(core0, ratio[:half], ratio[half:])[:, None]
    got = swap_core(send).astype(f32)
    pair = keep[0] + got[0] + ratio * (keep[1] + got[1])
    got = swap_chip(pair.astype(bf16))
    upstream = view_blocks(cotangent)
    after, scale_two, low = call(
        norm_kernel,
        [((half, D), f32), ((half, 1), f32), ((half, D), bf16)],
        idx, *source, pair, got, gain_b,
        us=3.8,
    )
    normed_two, up_one, act, grad_gu, keep, send = call(
        mlp_kernel,
        [((length, D), bf16)] * 2
        + [((length, 512), bf16), ((length, 1024), bf16), ((half, D), f32), ((half, D), bf16)],
        idx, low, swap_core(low), *upstream, w_mlp,
        us=8,
    )
    pair, got, act = token_pair(keep, send, act)
    (grads,) = call(
        grads_kernel, [((D, 1536), bf16)], up_one, act, normed_two, grad_gu, us=5.2,
    )
    got, _ = lax.optimization_barrier((got, grads))
    parts_mlp = send_rows(grads)
    grad_mid, low, gain_two = call(
        norm_back_kernel,
        [((half, D), f32), ((half, D), bf16), ((1, D), f32)],
        idx, *upstream, pair, got, after, scale_two, gain_b,
        us=1.0,
    )
    up_two, grad_attn, scaled, inner, grad_ssm_gain, scale_ssm, mixed = call(
        mix_back_kernel,
        [((length, D), bf16), (token128, f32), ((length, 384), f32), ((8, length), f32), ((1, 384), f32)]
        + [((length, 1), f32), ((length, 512), bf16)],
        idx, low, swap_core(low), weight_mix, attn, gated, ssq, ssm_gain,
        us=1.0,
    )
    inner = sum_col(inner)
    dquery, dkey, dvalue = call(
        attention_back_kernel,
        [(token128, bf16), (token128, f32), (token128, f32)],
        grad_attn, attn, probs, qrot, krot, value, cosine, sine, tok,
        us=4.4,
    )
    dproj, dstep, keep, send, small, conv_x = call(
        ssm_back_kernel,
        [((length, 896), bf16), (token128, bf16), ((2,) + token128, f32), ((2,) + token128, bf16), ((8, 128), f32), ((8, 384), f32)],
        idx, scaled, gated, ssm, scale_ssm, inner, dquery, gates, inners, raw, xin, step, cumc, cumr,
        state_b, state_c, tok, seg, heads, skip, cweight, cbias, dkey, dvalue,
        us=6,
    )
    grad_sent, up_two = feature_sum(keep, send, up_two)
    (grads,) = call(
        grads_kernel, [((D, 1024), bf16)], up_two, mixed, normed, dproj, us=4.3,
    )
    held = grads
    grads, parts_mlp = lax.optimization_barrier((grads, parts_mlp))
    parts_mix = send_rows(grads)
    grad_sent, _ = lax.optimization_barrier((grad_sent, held))
    late, conv_s, gain_one, keep, send = call(
        in_back_kernel,
        [((length, 256), bf16), ((8, 128), f32), ((1, D), f32), ((2, length, 256), f32), ((2, length, 256), bf16)],
        idx, dproj, dstep, grad_sent, tile_in, tok, cweight, cbias, weight_mix, weight_rest,
        *source, scale_one, gain_a, grad_mid,
        scratch=[((length, D), f32)],
        us=3,
    )
    gain_grads = jnp.concatenate([gain_one, 0.5 * gain_two], 0)
    near, far, diagonal = swap_core(gain_grads), swap_chip(gain_grads), swap_both(gain_grads)
    gain_grads = (gain_grads + near) + (far + diagonal)

    own = lax.dynamic_slice_in_dim(gain_grads, column * 256, 256, 1)
    grad_cweight = jnp.concatenate([conv_x[:CONV], conv_s[:CONV, HEAD:]], 1)
    grad_cbias = jnp.concatenate([conv_x[CONV], conv_s[CONV, HEAD:]])
    pieces = (own, grad_ssm_gain[0], small[:3, :6], grad_cweight, grad_cbias)
    flat = jnp.concatenate([piece.reshape(-1) for piece in pieces])
    flat = jnp.pad(flat, (0, shard * pad_cols - flat.shape[0])).astype(bf16)
    flat = jnp.pad(flat.reshape(shard, pad_cols), ((0, 0), (128 - pad_cols, 0)))
    (grads,) = call(
        late_grads_kernel, [((D, 640), bf16)], normed, dproj, late, flat,
        us=0.1,
    )
    act, grads = lax.optimization_barrier((act, grads))
    keep_down, send_down = call(
        down_kernel,
        [((2, length, 256), f32), ((2, length, 256), bf16)],
        idx, act, w_mlp, after,
        scratch=[((length, D), f32)],
        us=0.5,
    )
    held = lax.optimization_barrier((grads, parts_mix, parts_mlp, keep, send, keep_down, send_down))
    grads, parts_mix, parts_mlp, keep, send, keep_down, send_down = held
    grad_hidden = feature_sum(keep, send)
    hidden_out = feature_sum(keep_down, send_down).astype(bf16)
    parts_late = send_rows(grads)
    grads_mlp = sum_rows(parts_mlp, side)
    grads_mix = sum_rows(parts_mix, side)
    total = sum_rows(parts_late, side)
    late_cols = in_cols - 512
    flat = total[:, late_cols:].reshape(-1)
    out_small = []
    start = 0
    for piece in pieces:
        out_small.append(flat[start : start + piece.size].reshape((1,) + piece.shape))
        start += piece.size
    return (
        hidden_out,
        grad_hidden,
        jnp.concatenate([grads_mix[:, 512:], total[:, :late_cols]], 1)[None],
        grads_mix[:, :512].T[None],
        grads_mlp[None, :, 512:],
        grads_mlp[:, :512].T[None],
        *out_small,
    )


def solution(mesh):
    in_specs = (
        P("row", "col"),
        P("row"),
        P("row", "col"),
        P(None, "row", "col"),
        P(None, "col", "row"),
        P(None, "row", "col"),
        P(None, "col", "row"),
        P(None, None, "col"),
        P(None, "col"),
        P(None, None, "col"),
        P(None, None, "col"),
        P(None, "col"),
    )
    out_specs = (
        P("row", "col"),
        P("row", "col"),
        P(None, "row", "col"),
        P(None, "col", "row"),
        P(None, "row", "col"),
        P(None, "col", "row"),
        P(None, None, "col"),
        P(None, "col"),
        P(None, None, "col"),
        P(None, None, "col"),
        P(None, "col"),
    )
    return jax.shard_map(
        per_device, mesh=mesh, in_specs=in_specs, out_specs=out_specs, check_vma=False
    )
```

```python
import math

import jax
import jax.numpy as jnp
from jax import lax
from jax.experimental import pallas as pl
from jax.experimental.pallas import tpu as pltpu
from jax.sharding import PartitionSpec as P

D = 1024
Q_HEADS = 8
KV_HEADS = 2
HEAD = 64
SSM_HEADS = 24
SSM_HEAD = 64
STATE = 128
CONV = 4
FF = 2048
LAYERS = 1
CHUNK = 256
VMEM_BYTES = 60 * 1024 * 1024


epsilon = 1e-05
rope_base = 10000.0
contract_last = (((1,), (1,)), ((), ()))
contract_first = (((0,), (0,)), ((), ()))


def sequence_masks(segments):
    length = segments.shape[0]
    index = jnp.arange(length, dtype=jnp.int32)
    previous = jnp.concatenate([segments[:1], segments[:-1]])
    starts = jnp.where(segments != previous, index, 0)
    positions = (index - lax.cummax(starts, axis=0)).astype(jnp.float32)
    allowed = (segments[:, None] == segments[None, :]) & (index[:, None] >= index[None, :])
    shifted = []
    for shift in range(CONV):
        earlier = jnp.concatenate([jnp.full((shift,), -1, jnp.int32), segments[: length - shift]])
        shifted.append((earlier == segments).astype(jnp.float32))
    return (positions, allowed, jnp.stack(shifted))


def where_lane(shape, limit):
    return lax.broadcasted_iota(jnp.int32, shape, 1) < limit


def sigmoid(values):
    return 1.0 / (1.0 + jnp.exp(-values))


def softplus(values):
    return jnp.maximum(values, 0.0) + jnp.log1p(jnp.exp(-jnp.abs(values)))


def four_blocks(idx, own, by_chip, by_core, by_both):
    chip0 = idx[0] == 0
    core0 = idx[1] == 0
    first = jnp.where(chip0, own, by_chip)
    second = jnp.where(chip0, by_core, by_both)
    third = jnp.where(chip0, by_chip, own)
    fourth = jnp.where(chip0, by_both, by_core)
    return (
        jnp.where(core0, first, second),
        jnp.where(core0, second, first),
        jnp.where(core0, third, fourth),
        jnp.where(core0, fourth, third),
    )


def rotated(values, cosine, sine):
    lane = lax.broadcasted_iota(jnp.int32, values.shape, 1)
    other = jnp.where(lane % HEAD < HEAD // 2, pltpu.roll(values, 96, 1), pltpu.roll(values, 32, 1))
    return values * cosine + other * sine


def conv_pre(inner, weight, bias, valid):
    running = bias + weight[0:1] * inner * valid[:, 0:1]
    for shift in range(1, CONV):
        running = running + weight[shift : shift + 1] * pltpu.roll(inner, shift, 0) * valid[
            :, shift : shift + 1
        ]
    return running


def conv_back(grad, inner, weight, valid):
    length = inner.shape[0]
    total = weight[0:1] * (grad * valid[:, 0:1])
    taps = [jnp.sum(grad * valid[:, 0:1] * inner, axis=0, keepdims=True)]
    for shift in range(1, CONV):
        seen = grad * valid[:, shift : shift + 1]
        total = total + weight[shift : shift + 1] * pltpu.roll(seen, length - shift, 0)
        taps.append(jnp.sum(seen * pltpu.roll(inner, shift, 0), axis=0, keepdims=True))
    return (total, taps, jnp.sum(grad, axis=0, keepdims=True))


def silu_slope(values, sig):
    return sig * (1.0 + values * (1.0 - sig))


def dot32(left, right, dims=(((1,), (0,)), ((), ()))):
    return lax.dot_general(left, right, dims, preferred_element_type=jnp.float32)


def exact(left, right):
    return lax.dot_general(
        left,
        right,
        (((1,), (0,)), ((), ())),
        precision=lax.Precision.HIGHEST,
        preferred_element_type=jnp.float32,
    )


def triangle(length, reverse=False):
    first = lax.broadcasted_iota(jnp.int32, (length, length), 0)
    second = lax.broadcasted_iota(jnp.int32, (length, length), 1)
    return jnp.where(second >= first if reverse else first >= second, 1.0, 0.0)


def head_sums(width):
    lane = lax.broadcasted_iota(jnp.int32, (width, 128), 0) // SSM_HEAD
    head = lax.broadcasted_iota(jnp.int32, (width, 128), 1)
    return jnp.where(lane == head, 1.0, 0.0)


def per_head(columns, tile, shape):
    return jnp.where(
        where_lane(shape, SSM_HEAD),
        jnp.broadcast_to(columns[:, 2 * tile : 2 * tile + 1], shape),
        jnp.broadcast_to(columns[:, 2 * tile + 1 : 2 * tile + 2], shape),
    )


def chunk_allowed(tok, seg, start, count):
    rows = tok.shape[0]
    time = lax.broadcasted_iota(jnp.int32, (rows, count), 0) + start
    source = lax.broadcasted_iota(jnp.int32, (rows, count), 1)
    return (tok[:, 4:5] == seg[0:1, :count]) & (time >= source)


def table_kernel(seg, params, tok_out, cosine_out, sine_out, heads_out, skip_out):
    length = seg.shape[1]
    shape = (length, 128)
    column = row_to_column(seg[...])
    time = lax.broadcasted_iota(jnp.int32, (length, 1), 0)
    allowed = chunk_allowed(jnp.broadcast_to(column, (length, 8)), seg[...], 0, length)
    positions = jnp.sum(jnp.where(allowed, 1.0, 0.0), axis=1, keepdims=True) - 1.0
    lane = lax.broadcasted_iota(jnp.int32, shape, 1)
    wide = jnp.broadcast_to(column, shape)
    tok = jnp.where(lane == 4, wide, 0.0)
    for shift in range(CONV):
        same = wide == (pltpu.roll(wide, shift, 0) if shift else wide)
        tok = jnp.where((lane == shift) & same & (time >= shift), 1.0, tok)
    tok_out[...] = tok
    slot = (lane % (HEAD // 2)).astype(jnp.float32)
    angle = positions * jnp.exp(slot * (-2.0 * math.log(rope_base) / HEAD))
    cosine_out[...] = jnp.cos(angle)
    sine = jnp.sin(angle)
    sine_out[...] = jnp.where(lane % HEAD < HEAD // 2, -sine, sine)
    heads_out[...] = jnp.zeros(heads_out.shape, jnp.float32)
    heads_out[0:3, 0:6] = params[...]
    lane = lax.broadcasted_iota(jnp.int32, skip_out.shape, 1) // SSM_HEAD
    skip = jnp.zeros(skip_out.shape, jnp.float32)
    for head in range(params.shape[1]):
        skip = jnp.where(lane == head, params[1:2, head : head + 1], skip)
    skip_out[...] = skip


def in_kernel(
    idx, own, by_chip, by_core, by_both, gain, weight, cweight, cbias, tok,
    normed_out, scale_out, inner_out, tile_out, raw_out, xin_out, sent_out,
):
    source = jnp.concatenate(
        four_blocks(idx, own[...], by_chip[...], by_core[...], by_both[...]), 1
    ).astype(jnp.float32)
    scale = lax.rsqrt(jnp.sum(source * source, axis=1, keepdims=True) / D + epsilon)
    normed = (source * scale * gain[0:1]).astype(jnp.bfloat16)
    normed_out[...] = normed
    normed_out.send()
    scale_out[...] = scale
    proj = dot32(normed, weight[...])
    inner = proj[:, :512]
    inner_out[...] = proj[:, :384]
    inner_out.send()
    tile_out[...] = proj[:, 384:512]
    raw_out[...] = proj[:, 512:]
    pre = conv_pre(inner, cweight[...], cbias[0:1], tok[...])
    active = pre * sigmoid(pre)
    tile = inner[:, 384:]
    sent_out[...] = jnp.where(where_lane(tile.shape, HEAD), tile, active[:, 384:]).astype(
        jnp.bfloat16
    )
    xin_out[...] = active[:, :384]


def ssm_kernel(
    idx, own, by_chip, by_core, by_both, raw, heads, xin, tok, seg, normed, weight, skip,
    gated_out, gate_out, query_out, ssm_out, ssq_out, state_b_out, state_c_out, step_out, cumc_out, cumr_out,
):
    f32 = jnp.float32
    bf16 = jnp.bfloat16
    length = raw.shape[0]
    blocks = four_blocks(
        idx, own[...].astype(f32), by_chip[...].astype(f32), by_core[...].astype(f32),
        by_both[...].astype(f32),
    )
    shape = (length, 128)
    left = where_lane(shape, HEAD)
    state_b = jnp.where(left, pltpu.roll(blocks[0], 64, 1), blocks[1]).astype(bf16)
    state_c = jnp.where(left, pltpu.roll(blocks[2], 64, 1), blocks[3]).astype(bf16)
    state_b_out[...] = state_b
    state_c_out[...] = state_c
    step = softplus(raw[...] + heads[2:3])
    step_out[...] = step
    cum = exact(triangle(length), step * -jnp.exp(heads[0:1]))
    cumc_out[...] = cum
    cumr = cum.T[:8]
    cumr_out[...] = cumr
    xin_all = xin[...]
    tiles = xin_all.shape[1] // 128
    inputs = [
        (per_head(step, tile, shape) * xin_all[:, 128 * tile : 128 * tile + 128]).astype(bf16)
        for tile in range(tiles)
    ]
    gates = dot32(normed[...], weight[:, 512:])
    query_out[...] = gates[:, :128]
    gates = gates[:, 128:]
    gate_out[...] = gates
    gate_out.send()
    half = min(CHUNK, length)
    for start in range(0, length, half):
        count = start + half
        rows = slice(start, count)
        allowed = chunk_allowed(tok[rows, :], seg[...], start, count)
        first = where_lane((half, 128), HEAD)
        gram = dot32(state_c[rows], state_b[:count], contract_last)
        total = jnp.zeros((half, 128), f32)
        for tile in range(tiles):
            lanes = slice(128 * tile, 128 * tile + 128)
            outs = []
            for head in (2 * tile, 2 * tile + 1):
                diff = cum[rows, head : head + 1] - cumr[head : head + 1, :count]
                mixing = jnp.exp(jnp.where(allowed, diff, -1e30)) * gram
                outs.append(dot32(mixing.astype(bf16), inputs[tile][:count]))
            ssm = jnp.where(first, outs[0], outs[1]) + skip[0:1, lanes] * xin_all[rows, lanes]
            ssm_out[rows, lanes] = ssm
            gate = gates[rows, lanes]
            gated = ssm * (gate * sigmoid(gate))
            gated_out[rows, lanes] = gated
            total = total + gated * gated
        ssq_out[:, rows] = lax.dot_general(
            jnp.ones((8, 128), f32),
            total,
            contract_last,
            precision=lax.Precision.HIGHEST,
            preferred_element_type=f32,
        )


def attention_kernel(
    idx, own, by_chip, by_core, by_both, query, cosine, sine, tok, seg, gated, gain, weight,
    attn_out, probs_out, qrot_out, krot_out, value_out, keep_out, send_out, scaled,
):
    f32 = jnp.float32
    bf16 = jnp.bfloat16
    length = query.shape[0]
    blocks = four_blocks(
        idx, own[...].astype(f32), by_chip[...].astype(f32), by_core[...].astype(f32),
        by_both[...].astype(f32),
    )
    chip0 = idx[0] == 0
    left = where_lane((length, 128), HEAD)
    keys = jnp.where(chip0, blocks[0], blocks[1])
    values = jnp.where(chip0, blocks[2], blocks[3])
    keys = jnp.where(left, keys, pltpu.roll(keys, 64, 1))
    values = jnp.where(left, values, pltpu.roll(values, 64, 1)).astype(bf16)
    krot = rotated(keys, cosine[...], sine[...]).astype(bf16)
    qrot = rotated(query[...], cosine[...], sine[...]).astype(bf16)
    value_out[...] = values
    krot_out[...] = krot
    qrot_out[...] = qrot
    half = min(CHUNK, length)
    for start in range(0, length, half):
        count = start + half
        rows = slice(start, count)
        allowed = chunk_allowed(tok[rows, :], seg[...], start, count)
        first = where_lane((half, 128), HEAD)
        outs = []
        for head in range(2):
            mine = jnp.where(first == (head == 0), qrot[rows].astype(f32), 0.0).astype(bf16)
            scores = dot32(mine, krot[:count], contract_last) * HEAD ** (-0.5)
            scores = jnp.where(allowed, scores, -1e30)
            weights = jnp.exp(scores - jnp.max(scores, axis=1, keepdims=True))
            probs = (weights / jnp.sum(weights, axis=1, keepdims=True)).astype(bf16)
            probs_out[head, rows, :count] = probs
            outs.append(dot32(probs, values[:count]))
        attn_out[rows, :] = jnp.where(first, outs[0], outs[1]).astype(bf16)
    probs_out.send()
    scaled[...] = (gated[...] * gain[0:1]).astype(bf16)
    core = idx[1]
    for place, rows in ((0, half_rows(1 - core, length)), (1, half_rows(core, length))):
        for part, source, lanes in ((0, attn_out, (0, 128)), (1, scaled, (128, 512))):
            product = dot32(source[rows, :], weight[:, lanes[0] : lanes[1]], contract_last)
            if place == 0:
                send_out[part, :, :] = product.astype(bf16)
            else:
                keep_out[part, :, :] = product
        if place == 0:
            send_out.send()


def attention_back_kernel(
    grad, attn, probs, qrot, krot, value, cosine, sine, tok,
    dquery_out, dkey_out, dvalue_out,
):
    f32 = jnp.float32
    bf16 = jnp.bfloat16
    length = grad.shape[0]
    shape = (length, 128)
    lane0 = where_lane(shape, HEAD)
    dkey = [jnp.zeros(shape, f32), jnp.zeros(shape, f32)]
    dvalue = jnp.zeros(shape, f32)
    half = min(CHUNK, length)
    dquery = []
    keyparts = []
    valueparts = []
    for start in range(0, length, half):
        count = start + half
        rows = slice(start, count)
        first = where_lane((half, 128), HEAD)
        dout = grad[rows, :]
        product = dout * attn[rows, :].astype(f32)
        outs = []
        dk = []
        dv = []
        for head in range(2):
            mine = first == (head == 0)
            dhead = jnp.where(mine, dout, 0.0).astype(bf16)
            query = jnp.where(mine, qrot[rows, :].astype(f32), 0.0).astype(bf16)
            part = probs[head, rows, :count]
            dprob = dot32(dhead, value[:count, :], contract_last)
            inner = jnp.sum(jnp.where(mine, product, 0.0), axis=1, keepdims=True)
            dscore = (part.astype(f32) * (dprob - inner) * HEAD ** (-0.5)).astype(bf16)
            outs.append(dot32(dscore, krot[:count, :]))
            dk.append(dot32(dscore, query, contract_first))
            dv.append(dot32(part, dhead, contract_first))
        dquery.append(jnp.where(first, outs[0], outs[1]))
        keyparts.append(dk[0] + dk[1])
        valueparts.append(dv[0] + dv[1])

    def gathered(parts):
        total = parts[-1]
        for part in parts[:-1]:
            pad = jnp.zeros((length - part.shape[0], 128), f32)
            total = total + jnp.concatenate([part, pad], 0)
        return total + pltpu.roll(total, 64, 1)

    back = -sine[...]
    dquery_out[...] = rotated(jnp.concatenate(dquery, 0), cosine[...], back).astype(bf16)
    dkey_out[...] = rotated(gathered(keyparts), cosine[...], back)
    dvalue_out[...] = gathered(valueparts)


def ssm_back_kernel(
    idx, scaled, gated, ssm, scale_ssm, inner, dquery, gates, inners, raw, xin, step, cumc, cumr, state_b, state_c,
    tok, seg, heads, skip, cweight, cbias, dkey, dvalue,
    dproj_out, dstep_out, keep_out, send_out, small_out, conv_out,
):
    f32 = jnp.float32
    bf16 = jnp.bfloat16
    length = xin.shape[0]
    shape = (length, 128)
    tiles = xin.shape[1] // 128
    scale = scale_ssm[...]
    shrink = scale * scale * scale * row_to_column(inner[...]) / (SSM_HEADS * SSM_HEAD)
    dproj_out[:, :128] = dquery[...]
    step_all = step[...]
    left = where_lane(shape, HEAD)
    grads = []
    grads_low = []
    inputs = []
    for tile in range(tiles):
        lanes = slice(128 * tile, 128 * tile + 128)
        gate = gates[:, lanes]
        sig = sigmoid(gate)
        grad_gated = scale * scaled[:, lanes] - gated[:, lanes] * shrink
        dproj_out[:, 128 + 128 * tile : 256 + 128 * tile] = (grad_gated * ssm[:, lanes] * silu_slope(gate, sig)).astype(bf16)
        grad = grad_gated * gate * sig
        grads.append(grad)
        grads_low.append(grad.astype(bf16))
        inputs.append((per_head(step_all, tile, shape) * xin[:, lanes]).astype(bf16))
    half = min(CHUNK, length)
    dinputs = [[] for _ in range(tiles)]
    dstate_b = []
    dstate_c = []
    for start in range(0, length, half):
        count = start + half
        rows = slice(start, count)
        allowed = chunk_allowed(tok[rows, :], seg[...], start, count)
        first = where_lane((half, 128), HEAD)
        gram = dot32(state_c[rows, :], state_b[:count, :], contract_last)
        dgram = jnp.zeros((half, count), f32)
        for tile in range(tiles):
            pair = []
            low = grads_low[tile][rows]
            for head in (2 * tile, 2 * tile + 1):
                diff = cumc[rows, head : head + 1] - cumr[head : head + 1, :count]
                decay = jnp.exp(jnp.where(allowed, diff, -1e30))
                mixing = (decay * gram).astype(bf16)
                mine = jnp.where(first == (head % 2 == 0), low.astype(f32), 0.0).astype(bf16)
                dgram = dgram + decay * dot32(mine, inputs[tile][:count], contract_last)
                pair.append(dot32(mixing, low, contract_first))
            dinputs[tile].append(jnp.where(where_lane((count, 128), HEAD), pair[0], pair[1]))
        dgram = dgram.astype(bf16)
        dstate_c.append(dot32(dgram, state_b[:count, :]))
        dstate_b.append(dot32(dgram, state_c[rows, :], contract_first))

    def gathered(parts):
        total = parts[-1]
        for part in parts[:-1]:
            pad = jnp.zeros((length - part.shape[0], 128), f32)
            total = total + jnp.concatenate([part, pad], 0)
        return total

    valid = tok[...]
    balance = jnp.zeros(shape, f32)
    dstep = jnp.zeros(shape, f32)
    dskip = jnp.zeros((1, 128), f32)
    sums = head_sums(128 * tiles)
    for tile in range(tiles):
        lanes = slice(128 * tile, 128 * tile + 128)
        dinput = gathered(dinputs[tile])
        own = xin[:, lanes]
        plain = ssm[:, lanes] - skip[0:1, lanes] * own
        select = sums[128 * tile : 128 * tile + 128]
        balance = balance + exact(
            grads_low[tile].astype(f32) * plain - inputs[tile].astype(f32) * dinput, select
        )
        dstep = dstep + exact(dinput * own, select)
        dskip = dskip + exact(
            jnp.broadcast_to(jnp.sum(grads[tile] * own, axis=0, keepdims=True), (8, 128)), select
        )[0:1]
        dxin = skip[0:1, lanes] * grads[tile] + per_head(step_all, tile, shape) * dinput
        source = inners[:, lanes]
        weight = cweight[:, lanes]
        pre = conv_pre(source, weight, cbias[0:1, lanes], valid)
        dpre = dxin * silu_slope(pre, sigmoid(pre))
        dsource, taps, dbias = conv_back(dpre, source, weight, valid)
        dproj_out[:, 512 + 128 * tile : 640 + 128 * tile] = dsource.astype(bf16)
        for shift in range(CONV):
            conv_out[shift : shift + 1, lanes] = taps[shift]
        conv_out[CONV : CONV + 1, lanes] = dbias
    rate = -jnp.exp(heads[0:1])
    dlog = exact(triangle(length, True), balance)
    dstep = (dstep + dlog * rate) * sigmoid(raw[...] + heads[2:3])
    dstep = jnp.where(where_lane(shape, SSM_HEADS // 4), dstep, 0.0)
    dstep_out[...] = dstep.astype(bf16)
    small_out[0:1, :] = jnp.sum(dlog * step_all, axis=0, keepdims=True) * rate
    small_out[1:2, :] = dskip
    small_out[2:3, :] = jnp.sum(dstep, axis=0, keepdims=True)
    small_out[3:8, :] = jnp.zeros((5, 128), f32)
    dstate_b = gathered(dstate_b)
    dstate_c = jnp.concatenate(dstate_c, 0)
    chip0 = idx[0] == 0
    core0 = idx[1] == 0
    none = jnp.zeros(shape, f32)
    dkey0 = jnp.where(chip0, dkey[...], none)
    dkey1 = jnp.where(chip0, none, dkey[...])
    dvalue0 = jnp.where(chip0, dvalue[...], none)
    dvalue1 = jnp.where(chip0, none, dvalue[...])
    pieces = (
        jnp.where(left, dkey0, pltpu.roll(dstate_b, 64, 1)),
        jnp.where(left, dkey1, dstate_b),
        jnp.where(left, dvalue0, pltpu.roll(dstate_c, 64, 1)),
        jnp.where(left, dvalue1, dstate_c),
    )
    near = (jnp.where(core0, pieces[0], pieces[1]), jnp.where(core0, pieces[2], pieces[3]))
    away = (jnp.where(core0, pieces[1], pieces[0]), jnp.where(core0, pieces[3], pieces[2]))
    keep_out[0, :, :] = jnp.where(chip0, near[0], near[1])
    keep_out[1, :, :] = jnp.where(chip0, near[1], near[0])
    send_out[0, :, :] = jnp.where(chip0, away[0], away[1]).astype(bf16)
    send_out[1, :, :] = jnp.where(chip0, away[1], away[0]).astype(bf16)


def row_to_column(row):
    return jnp.broadcast_to(row[0:1], (128, row.shape[1])).T[:, 0:1]


def half_rows(core, length):
    return pl.ds(pl.multiple_of(core * (length // 2), length // 2), length // 2)


def block_halves(idx, blocks):
    rows = half_rows(idx[1], blocks[0].shape[0])
    return jnp.concatenate(four_blocks(idx, *(block[rows, :] for block in blocks)), 1).astype(
        jnp.float32
    )


def norm_kernel(idx, own, by_chip, by_core, by_both, pair, got, gain, after_out, scale_out, low_out):
    after = (
        block_halves(idx, (own, by_chip, by_core, by_both))
        + pair[...]
        + got[...].astype(jnp.float32)
    )
    scale = lax.rsqrt(jnp.sum(after * after, axis=1, keepdims=True) / D + epsilon)
    after_out[...] = after
    scale_out[...] = scale
    low_out[...] = (after * scale * gain[0:1]).astype(jnp.bfloat16)


def joined(idx, near, away):
    core0 = idx[1] == 0
    near, away = near[...], away[...]
    return jnp.concatenate([jnp.where(core0, near, away), jnp.where(core0, away, near)], 0)


def mlp_kernel(
    idx, near, away, own, by_chip, by_core, by_both, weights,
    normed_out, up_out, act_out, grad_out, keep_out, send_out,
):
    length = own.shape[0]
    cols = weights.shape[1] // 3
    normed = joined(idx, near, away)
    normed_out[...] = normed
    normed_out.send()
    upstream = jnp.concatenate(
        four_blocks(idx, own[...], by_chip[...], by_core[...], by_both[...]), 1
    )
    up_out[...] = upstream
    up_out.send()
    both = dot32(normed, weights[:, : 2 * cols])
    gate = both[:, :cols]
    upper = both[:, cols:]
    sig = sigmoid(gate)
    act_out[...] = (gate * sig * upper).astype(jnp.bfloat16)
    grad = dot32(upstream, weights[:, 2 * cols :])
    grad_out[:, :cols] = (grad * upper * silu_slope(gate, sig)).astype(jnp.bfloat16)
    grad_out[:, cols:] = (grad * gate * sig).astype(jnp.bfloat16)
    core = idx[1]
    away = grad_out[half_rows(1 - core, length), :]
    send_out[...] = dot32(away, weights[:, : 2 * cols], contract_last).astype(jnp.bfloat16)
    send_out.send()
    keep_out[...] = dot32(
        grad_out[half_rows(core, length), :], weights[:, : 2 * cols], contract_last
    )


def norm_back_kernel(
    idx, own, by_chip, by_core, by_both, keep, near, got, after, scale, gain,
    grad_out, low_out, gain_out,
):
    partial = keep[...] + near[...].astype(jnp.float32) + got[...].astype(jnp.float32)
    source = after[...]
    r = scale[...]
    scaled = partial * gain[0:1]
    inner = jnp.sum(scaled * source, axis=1, keepdims=True)
    grad = (
        block_halves(idx, (own, by_chip, by_core, by_both))
        + r * scaled
        - source * (r * r * r * inner / D)
    )
    grad_out[...] = grad
    low_out[...] = grad.astype(jnp.bfloat16)
    gain_out[...] = jnp.sum(partial * source * r, axis=0, keepdims=True)


def mix_back_kernel(
    idx, near, away, weight, attn, gated, total, gain,
    up_out, attn_out, scaled_out, inner_out, gain_out, scale_out, mixed_out,
):
    upstream = joined(idx, near, away)
    up_out[...] = upstream
    up_out.send()
    grad = dot32(upstream, weight[:, :512])
    attn_out[...] = grad[:, :128]
    grad = grad[:, 128:]
    scaled = grad * gain[0:1]
    scaled_out[...] = scaled
    source = gated[...]
    scale = lax.rsqrt(row_to_column(total[...]) / (SSM_HEADS * SSM_HEAD) + epsilon)
    scale_out[...] = scale
    product = scaled * source
    inner_out[...] = lax.dot_general(
        jnp.ones((8, product.shape[1]), jnp.float32),
        product,
        contract_last,
        precision=lax.Precision.HIGHEST,
        preferred_element_type=jnp.float32,
    )
    normal = source * scale
    gain_out[...] = jnp.sum(grad * normal, axis=0, keepdims=True)
    mixed_out[:, :128] = attn[...]
    mixed_out[:, 128:] = (normal * gain[0:1]).astype(jnp.bfloat16)


def feature_blocks(idx, total, keep_out, send_out):
    chip, core = idx[0], idx[1]
    for place, way in ((0, chip), (1, 1 - chip)):
        near = pl.multiple_of((2 * way + core) * 256, 256)
        away = pl.multiple_of((2 * way + 1 - core) * 256, 256)
        keep_out[place, :, :] = total[:, pl.ds(near, 256)]
        send_out[place, :, :] = total[:, pl.ds(away, 256)].astype(jnp.bfloat16)


def add_residual(idx, total, resid):
    rows = half_rows(idx[1], total.shape[0])
    lanes = pl.ds(pl.multiple_of(idx[0] * (D // 2), D // 2), D // 2)
    total[rows, lanes] = total[rows, lanes] + resid[:, lanes]


def down_kernel(idx, act, weight, resid, keep_out, send_out, total):
    total[...] = dot32(act[...], weight[:, 1024:], contract_last)
    add_residual(idx, total, resid)
    feature_blocks(idx, total, keep_out, send_out)


def in_back_kernel(
    idx, keep, got, far, tile_in, tok, cweight, cbias, dproj, dstep, weight_qz, weight_rest,
    own, by_chip, by_core, by_both, scale, gain, grad_mid,
    late_out, conv_out, gain_out, keep_out, send_out, total,
):
    inner = tile_in[...]
    taps_in = cweight[:, 384:]
    valid = tok[...]
    pre = conv_pre(inner, taps_in, cbias[0:1, 384:], valid)
    grad = keep[0] + got[0].astype(jnp.float32) + far[...].astype(jnp.float32)
    dpre = grad * silu_slope(pre, sigmoid(pre))
    dinner, taps, dbias = conv_back(dpre, inner, taps_in, valid)
    for shift in range(CONV):
        conv_out[shift : shift + 1, :] = taps[shift]
    conv_out[CONV : CONV + 1, :] = dbias
    conv_out[CONV + 1 :, :] = jnp.zeros((7 - CONV, 128), jnp.float32)
    tile = jnp.where(where_lane(grad.shape, HEAD), grad, dinner).astype(jnp.bfloat16)
    late = jnp.concatenate([tile, dstep[...]], 1)
    late_out[...] = late
    partial = dot32(dproj[:, :512], weight_qz[:, 512:], contract_last) + dot32(
        jnp.concatenate([dproj[:, 512:], late], 1), weight_rest[...], contract_last
    )
    source = jnp.concatenate(
        four_blocks(idx, own[...], by_chip[...], by_core[...], by_both[...]), 1
    ).astype(jnp.float32)
    r = scale[...]
    scaled = partial * gain[0:1]
    dots = jnp.sum(scaled * source, axis=1, keepdims=True)
    total[...] = r * scaled - source * (r * r * r * dots / D)
    gain_out[...] = jnp.sum(partial * source * r, axis=0, keepdims=True)
    add_residual(idx, total, grad_mid)
    feature_blocks(idx, total, keep_out, send_out)


def grads_kernel(first, second, third, fourth, out):
    cols = second.shape[1]
    more = out.shape[1] - cols
    out[:, :cols] = dot32(first[...], second[...], contract_first).astype(jnp.bfloat16)
    out[:, cols:] = dot32(third[...], fourth[:, :more], contract_first).astype(jnp.bfloat16)


def late_grads_kernel(normed, dproj, late, small, out):
    right = jnp.concatenate([dproj[:, 512:], late[...]], 1)
    out[...] = dot32(normed[...], right, contract_first).astype(jnp.bfloat16)
    shard = small.shape[0]
    first = where_lane((shard, 128), 6)
    for start in range(0, out.shape[0], shard):
        rows = slice(start, start + shard)
        out[rows, 512:] = jnp.where(
            first, out[rows, 512:].astype(jnp.float32), small[...].astype(jnp.float32)
        ).astype(jnp.bfloat16)


class Fetch:
    def __init__(self, copy, ref):
        self.copy, self.ref, self.shape, self.open = copy, ref, ref.shape, True
        copy.start()

    def wait(self):
        if self.open:
            self.open = False
            self.copy.wait()

    def __getitem__(self, at):
        self.wait()
        return self.ref[at]


class Store:
    def __init__(self, copy, ref):
        self.copy, self.ref, self.shape, self.open = copy, ref, ref.shape, True

    def __setitem__(self, at, value):
        self.ref[at] = value

    def __getitem__(self, at):
        return self.ref[at]

    def send(self):
        if self.open:
            self.open = False
            self.copy.start()


def call(body, outs, *args, scratch=(), us=1.0, columns=()):
    scalars = sum(a.dtype == jnp.int32 for a in args)
    arrays = args[scalars:]
    columns = dict(columns)
    n_in, n_out = len(arrays), len(outs)

    def kernel(*refs):
        first = refs[:scalars]
        refs = refs[scalars:]
        far_in, far_out = refs[:n_in], refs[n_in : n_in + n_out]
        refs = refs[n_in + n_out :]
        near_in, near_out = refs[:n_in], refs[n_in : n_in + n_out]
        *rest, sems = refs[n_in + n_out :]
        fetches = [
            Fetch(
                pltpu.make_async_copy(
                    far.at[:, slice(*columns[i])] if i in columns else far,
                    near.at[:, slice(*columns[i])] if i in columns else near,
                    sems.at[i],
                ),
                near,
            )
            for i, (far, near) in enumerate(zip(far_in, near_in))
        ]
        stores = [
            Store(pltpu.make_async_copy(near, far, sems.at[n_in + i]), near)
            for i, (near, far) in enumerate(zip(near_out, far_out))
        ]
        body(*first, *fetches, *stores, *rest)
        for item in fetches:
            item.wait()
        for item in stores:
            item.send()
        for item in stores:
            item.copy.wait()

    hbm = pl.BlockSpec(memory_space=pltpu.HBM)
    return pl.pallas_call(
        kernel,
        out_shape=[jax.ShapeDtypeStruct(s, t) for s, t in outs],
        in_specs=[pl.BlockSpec(memory_space=pltpu.SMEM)] * scalars + [hbm] * n_in,
        out_specs=[hbm] * n_out,
        scratch_shapes=[pltpu.VMEM(a.shape, a.dtype) for a in arrays]
        + [pltpu.VMEM(s, t) for s, t in outs]
        + [pltpu.VMEM(*s) for s in scratch]
        + [pltpu.SemaphoreType.DMA((n_in + n_out,))],
        compiler_params=pltpu.CompilerParams(vmem_limit_bytes=VMEM_BYTES),
        cost_estimate=pl.CostEstimate(
            flops=int(us * 1.15e9), bytes_accessed=int(us * 3.69e6), transcendentals=0
        ),
    )(*args)


def swap_core(values):
    return lax.ppermute(values, "col", [(0, 1), (1, 0), (2, 3), (3, 2)])


def swap_chip(values):
    return lax.ppermute(values, "col", [(0, 2), (2, 0), (1, 3), (3, 1)])


def swap_both(values):
    return lax.ppermute(values, "col", [(0, 3), (3, 0), (1, 2), (2, 1)])


def swap_half(values):
    return lax.ppermute(values, "row", [(i, i ^ 1) for i in range(lax.axis_size("row"))])


def sum_col(values):
    near, far, diagonal = swap_core(values), swap_chip(values), swap_both(values)
    return (values + near) + (far + diagonal)


def view_blocks(block):
    by_core = swap_core(block)
    by_chip = swap_chip(block)
    return (block, by_chip, by_core, swap_core(by_chip))


def token_pair(keep, send, after):
    near = swap_core(send)
    low = (keep + near.astype(jnp.float32)).astype(jnp.bfloat16)
    low, after = lax.optimization_barrier((low, after))
    return (near, swap_chip(low), after)


def feature_sum(keep, send):
    got = swap_core(send)
    far = swap_chip((keep[1] + got[1].astype(jnp.float32)).astype(jnp.bfloat16))
    return keep[0] + got[0].astype(jnp.float32) + far.astype(jnp.float32)


def plane_exchange(values):
    rows = lax.axis_size("row")
    groups = [list(range(0, rows, 2)), list(range(1, rows, 2))]
    return lax.all_to_all(values, "row", 0, 0, axis_index_groups=groups, tiled=True)


def gather_pair(pair):
    count = lax.axis_size("row") // 2
    full = plane_exchange(jnp.broadcast_to(pair[None], (count,) + pair.shape))
    return full.reshape(-1, pair.shape[-1])


def send_rows(grad):
    count = lax.axis_size("row") // 2
    return plane_exchange(grad.reshape(count, grad.shape[0] // count, -1))


def sum_rows(parts, side):
    height = parts.shape[1] // 2
    part = jnp.sum(parts.astype(jnp.float32), axis=0)
    low, high = part[:height], part[height:]
    got = swap_half(jnp.where(side == 0, high, low).astype(jnp.bfloat16))
    return jnp.where(side == 0, low, high) + got.astype(jnp.float32)


def per_device(
    hidden_in,
    segment_ids,
    cotangent,
    w_in,
    w_out,
    w_gate_up,
    w_down,
    norm_gains,
    ssm_gain,
    head_params,
    conv_weight,
    conv_bias,
):
    rows = lax.axis_size("row")
    column = lax.axis_index("col")
    side = lax.axis_index("row") % 2
    idx = jnp.stack([column // 2, column % 2]).astype(jnp.int32)
    shard = w_in.shape[1]
    in_cols = w_in.shape[2]
    bf16 = jnp.bfloat16
    f32 = jnp.float32
    length = hidden_in.shape[0]
    half = length // 2

    source = view_blocks(hidden_in)
    gains = view_blocks(norm_gains[0])
    pad_cols = -in_cols % 128
    early_cols = 512
    first = jnp.pad(w_in[0, :, early_cols:], ((0, 0), (0, pad_cols)))
    rest = jnp.concatenate([w_out[0].T, w_in[0, :, :early_cols], w_gate_up[0], w_down[0].T], 1)
    other = swap_half(rest)
    spread = jnp.broadcast_to(first[None], (rows,) + first.shape)
    weight_rest = lax.all_to_all(spread, "row", 0, 0, tiled=True).reshape(D, -1)

    token128 = (length, 128)
    seg = segment_ids.astype(f32)[None, :]
    tok, cosine, sine, heads, skip = call(
        table_kernel,
        [(token128, f32)] * 3 + [((8, 128), f32), ((1, 384), f32)],
        seg, head_params[0],
        us=2,
    )
    gap = jnp.zeros((CONV, HEAD), f32)
    cweight = jnp.concatenate([conv_weight[0, :, :384], gap, conv_weight[0, :, 384:]], 1)
    cbias = jnp.concatenate([conv_bias[:, :384], gap[:1], conv_bias[:, 384:]], 1)
    chip0, core0 = idx[0] == 0, idx[1] == 0
    even = [jnp.where(core0, gains[i], gains[j]) for i, j in ((0, 2), (1, 3))]
    odd = [jnp.where(core0, gains[j], gains[i]) for i, j in ((0, 2), (1, 3))]
    gains = jnp.concatenate(
        [
            jnp.where(chip0, even[0], even[1]),
            jnp.where(chip0, odd[0], odd[1]),
            jnp.where(chip0, even[1], even[0]),
            jnp.where(chip0, odd[1], odd[0]),
        ],
        1,
    )

    rest = jnp.where(side == 0, jnp.stack([rest, other]), jnp.stack([other, rest]))
    tables = (
        weight_rest, rest, tok, seg, cosine, sine, heads, skip, cweight, cbias, gains, *source
    )
    tables = lax.optimization_barrier(tables)
    weight_rest, rest, tok, seg, cosine, sine, heads, skip, cweight, cbias, gains, *source = tables
    gain_a, gain_b = gains[0:1], gains[1:2]
    weight_mix = gather_pair(rest[:, :, :1024])
    normed, scale_one, inners, tile_in, raw, xin, sent = call(
        in_kernel,
        [((length, D), bf16), ((length, 1), f32)]
        + [((length, 384), f32), (token128, f32), (token128, f32), ((length, 384), f32), (token128, bf16)],
        idx, *source, gain_a, weight_rest, cweight, cbias, tok,
        us=5.5,
    )
    shared = view_blocks(sent)
    rest, weight_mix, *shared = lax.optimization_barrier((rest, weight_mix, *shared))
    w_mlp = gather_pair(rest[:, :, 1024:])
    gated, gates, query, ssm, ssq, state_b, state_c, step, cumc, cumr = call(
        ssm_kernel,
        [((length, 384), f32)] * 2
        + [(token128, f32), ((length, 384), f32), ((8, length), f32)]
        + [(token128, bf16)] * 2
        + [(token128, f32)] * 2
        + [((8, length), f32)],
        idx, *shared, raw, heads, xin, tok, seg, normed, weight_mix, skip,
        us=9,
        columns=((10, (512, 1024)),),
    )
    attn, probs, qrot, krot, value, keep, send = call(
        attention_kernel,
        [(token128, bf16), ((2, length, length), bf16)]
        + [(token128, bf16)] * 3
        + [((2, half, D), f32), ((2, half, D), bf16)],
        idx, *shared, query, cosine, sine, tok, seg, gated, ssm_gain, weight_mix,
        scratch=[((length, 384), bf16)],
        columns=((11, (0, 512)),),
        us=7,
    )
    ssq, keep = lax.optimization_barrier((sum_col(ssq), keep))
    ratio = lax.rsqrt(ssq[0] / (SSM_HEADS * SSM_HEAD) + epsilon)
    ratio = jnp.where(core0, ratio[:half], ratio[half:])[:, None]
    got = swap_core(send).astype(f32)
    pair = keep[0] + got[0] + ratio * (keep[1] + got[1])
    got = swap_chip(pair.astype(bf16))
    upstream = view_blocks(cotangent)
    after, scale_two, low = call(
        norm_kernel,
        [((half, D), f32), ((half, 1), f32), ((half, D), bf16)],
        idx, *source, pair, got, gain_b,
        us=3.8,
    )
    normed_two, up_one, act, grad_gu, keep, send = call(
        mlp_kernel,
        [((length, D), bf16)] * 2
        + [((length, 512), bf16), ((length, 1024), bf16), ((half, D), f32), ((half, D), bf16)],
        idx, low, swap_core(low), *upstream, w_mlp,
        us=8,
    )
    near, got, act = token_pair(keep, send, act)
    (grads,) = call(
        grads_kernel, [((D, 1536), bf16)], up_one, act, normed_two, grad_gu, us=5.2,
    )
    got, _ = lax.optimization_barrier((got, grads))
    parts_mlp = send_rows(grads)
    grad_mid, low, gain_two = call(
        norm_back_kernel,
        [((half, D), f32), ((half, D), bf16), ((1, D), f32)],
        idx, *upstream, keep, near, got, after, scale_two, gain_b,
        us=1.0,
    )
    up_two, grad_attn, scaled, inner, grad_ssm_gain, scale_ssm, mixed = call(
        mix_back_kernel,
        [((length, D), bf16), (token128, f32), ((length, 384), f32), ((8, length), f32), ((1, 384), f32)]
        + [((length, 1), f32), ((length, 512), bf16)],
        idx, low, swap_core(low), weight_mix, attn, gated, ssq, ssm_gain,
        columns=((2, (0, 512)),),
        us=1.0,
    )
    inner = sum_col(inner)
    dquery, dkey, dvalue = call(
        attention_back_kernel,
        [(token128, bf16), (token128, f32), (token128, f32)],
        grad_attn, attn, probs, qrot, krot, value, cosine, sine, tok,
        us=4.4,
    )
    dproj, dstep, keep, send, small, conv_x = call(
        ssm_back_kernel,
        [((length, 896), bf16), (token128, bf16), ((2,) + token128, f32), ((2,) + token128, bf16), ((8, 128), f32), ((8, 384), f32)],
        idx, scaled, gated, ssm, scale_ssm, inner, dquery, gates, inners, raw, xin, step, cumc, cumr,
        state_b, state_c, tok, seg, heads, skip, cweight, cbias, dkey, dvalue,
        us=2.5,
    )
    got = swap_core(send)
    far = (keep[1] + got[1].astype(f32)).astype(bf16)
    far, up_two = lax.optimization_barrier((far, up_two))
    far = swap_chip(far)
    (grads,) = call(
        grads_kernel, [((D, 1024), bf16)], up_two, mixed, normed, dproj, us=4.3,
    )
    held = grads
    grads, parts_mlp = lax.optimization_barrier((grads, parts_mlp))
    parts_mix = send_rows(grads)
    far, _ = lax.optimization_barrier((far, held))
    late, conv_s, gain_one, keep, send = call(
        in_back_kernel,
        [((length, 256), bf16), ((8, 128), f32), ((1, D), f32), ((2, length, 256), f32), ((2, length, 256), bf16)],
        idx, keep, got, far, tile_in, tok, cweight, cbias, dproj, dstep, weight_mix, weight_rest,
        *source, scale_one, gain_a, grad_mid,
        scratch=[((length, D), f32)],
        columns=((9, (512, 1024)),),
        us=14,
    )
    gain_grads = sum_col(jnp.concatenate([gain_one, 0.5 * gain_two], 0))

    own = lax.dynamic_slice_in_dim(gain_grads, column * 256, 256, 1)
    grad_cweight = jnp.concatenate([conv_x[:CONV], conv_s[:CONV, HEAD:]], 1)
    grad_cbias = jnp.concatenate([conv_x[CONV], conv_s[CONV, HEAD:]])
    pieces = (own, grad_ssm_gain[0], small[:3, :6], grad_cweight, grad_cbias)
    flat = jnp.concatenate([piece.reshape(-1) for piece in pieces])
    flat = jnp.pad(flat, (0, shard * pad_cols - flat.shape[0])).astype(bf16)
    flat = jnp.pad(flat.reshape(shard, pad_cols), ((0, 0), (128 - pad_cols, 0)))
    (grads,) = call(
        late_grads_kernel, [((D, 640), bf16)], normed, dproj, late, flat,
        us=5,
    )
    act, grads = lax.optimization_barrier((act, grads))
    keep_down, send_down = call(
        down_kernel,
        [((2, length, 256), f32), ((2, length, 256), bf16)],
        idx, act, w_mlp, after,
        scratch=[((length, D), f32)],
        us=0.5,
    )
    held = lax.optimization_barrier((grads, parts_mix, parts_mlp, keep, send, keep_down, send_down))
    grads, parts_mix, parts_mlp, keep, send, keep_down, send_down = held
    grad_hidden = feature_sum(keep, send)
    hidden_out = feature_sum(keep_down, send_down).astype(bf16)
    parts_late = send_rows(grads)
    grads_mlp = sum_rows(parts_mlp, side)
    grads_mix = sum_rows(parts_mix, side)
    total = sum_rows(parts_late, side)
    late_cols = in_cols - 512
    flat = total[:, late_cols:].reshape(-1)
    out_small = []
    start = 0
    for piece in pieces:
        out_small.append(flat[start : start + piece.size].reshape((1,) + piece.shape))
        start += piece.size
    return (
        hidden_out,
        grad_hidden,
        jnp.concatenate([grads_mix[:, 512:], total[:, :late_cols]], 1)[None],
        grads_mix[:, :512].T[None],
        grads_mlp[None, :, 512:],
        grads_mlp[:, :512].T[None],
        *out_small,
    )


def solution(mesh):
    in_specs = (
        P("row", "col"),
        P("row"),
        P("row", "col"),
        P(None, "row", "col"),
        P(None, "col", "row"),
        P(None, "row", "col"),
        P(None, "col", "row"),
        P(None, None, "col"),
        P(None, "col"),
        P(None, None, "col"),
        P(None, None, "col"),
        P(None, "col"),
    )
    out_specs = (
        P("row", "col"),
        P("row", "col"),
        P(None, "row", "col"),
        P(None, "col", "row"),
        P(None, "row", "col"),
        P(None, "col", "row"),
        P(None, None, "col"),
        P(None, "col"),
        P(None, None, "col"),
        P(None, None, "col"),
        P(None, "col"),
    )
    return jax.shard_map(
        per_device, mesh=mesh, in_specs=in_specs, out_specs=out_specs, check_vma=False
    )
```
